32 devices in a mesh: wide: 8 (over y, x, core), narrow: 4 (over z).
Axes of the slice: x: 2, y: 2, z: 4, core: 2. Of those that a mesh axis runs over, the one named last changes fastest.
Arguments:
- activations: bfloat16 [1024, 16384], P('wide', 'narrow'), may hold values from -30 to 30, as said below
- weight_tile: bfloat16 [16384, 16384], P('wide', 'narrow'), may hold values from -3 to 3
- codes: int32 [16384, 16384], P('wide', 'narrow'), may hold values from -8 to 7
- group_scales: float32 [16384, 128], P('wide', 'narrow'), may hold values from 0.02 to 0.2
- right_factor: bfloat16 [16384, 256], replicated, may hold values from -0.046875 to 0.046875
Outputs:
- residual_product: float32 [16384, 256], P(('wide', 'narrow'))
- gram: float32 [256, 256], replicated
- hessian_tiles: bfloat16 [16384, 16384], P('wide', 'narrow')
The draws below stay inside these ranges and needn't reach their ends.
Inputs may be any that keep to these rules, and one draw needn't show every extreme that they name: `activations`: each token's features are a product of a token scale, a feature scale and a value.
All inputs are finite; a program needn't handle non-finite values.
Results may differ from the reference program's by a relative error of at most 0.0049.
Values may be sent and summed in bfloat16 or wider, within the bound.
No kernel may reach another device: no remote copies, remote signals or barrier semaphores. Data moves between devices by JAX's collectives and lax.ppermute only.
A program may use at most 192 MiB of HBM per device.

```python
import math
import jax
import jax.numpy as jnp
from jax import lax

D = 16384
RANK = 256
GROUP = 128
TOKENS = 1024


def draw_activations(key, part):
    keys = jax.random.split(jax.random.fold_in(key, 71), 3)
    feature_scale = jnp.exp(jax.random.uniform(keys[0], (D,), jnp.float32, math.log(0.3), math.log(3.0)))
    token_scale = jnp.exp(jax.random.uniform(keys[1], (TOKENS,), jnp.float32, math.log(0.5), math.log(2.0)))
    base = jnp.clip(jax.random.normal(keys[2], (TOKENS, D), jnp.float32), -4.0, 4.0)
    return (base * token_scale[:, None] * feature_scale[None, :]).astype(jnp.bfloat16)


def plant(drawn, rng, least, largest):
    index_at = [jax.random.randint(jax.random.fold_in(rng, axis), (), 0, length) for axis, length in enumerate(drawn.shape)]
    longest = drawn.shape.index(max(drawn.shape))
    next_to = index_at[:longest] + [(index_at[longest] + 1) % drawn.shape[longest]] + index_at[longest + 1:]
    return drawn.at[tuple(index_at)].set(least).at[tuple(next_to)].set(largest)


def levels(stream_key, shape, pieces, smallest, largest):
    loudness = 1.0
    for dim, blocks in pieces:
        heights = jax.random.uniform(jax.random.fold_in(jax.random.fold_in(stream_key, 6), dim), (blocks,), jnp.float32, smallest / len(pieces), largest / len(pieces))
        loudness = loudness * jnp.repeat(jnp.exp(heights), shape[dim] // blocks).reshape((-1,) + (1,) * (len(shape) - 1 - dim))
    return loudness


def noise(stream_key, extent, width, reach, cuts=(), dtype=jnp.bfloat16):
    array = width * jax.random.normal(stream_key, extent, jnp.float32)
    if cuts:
        array = array * levels(stream_key, extent, cuts, -0.22, 0.18)
    return jnp.clip(array, -reach, reach).astype(dtype)


def setup_inputs(seed: int = 0) -> dict:
    seeds = jax.random.split(jax.random.key(seed), 6)
    activations = draw_activations(jax.random.fold_in(seeds[5], 71), 0)
    weight_tile = noise(seeds[1], (D, D), 0.5, 3.0, ((0, 8), (1, 4)))
    codes = plant(jax.random.randint(seeds[2], (D, D), -8, 8), jax.random.fold_in(seeds[2], 1), -8, 7).astype(jnp.int32)
    group_scales = jnp.clip(jnp.exp(math.log(0.2) - 2.3025851 * jax.random.uniform(seeds[3], (D, D // GROUP), jnp.float32) ** levels(seeds[3], (D, D // GROUP), ((0, 8), (1, 4)), -0.2, 0.2)), 0.02, 0.2)
    right_factor = noise(seeds[4], (D, RANK), D ** -0.5, 0.046875)
    return {"activations": activations, "weight_tile": weight_tile, "codes": codes, "group_scales": group_scales, "right_factor": right_factor}


def reference(activations, weight_tile, codes, group_scales, right_factor):
    hessian = lax.dot_general(activations, activations, (((0,), (0,)), ((), ())), preferred_element_type=jnp.float32) / TOKENS
    hessian_tiles = hessian.astype(jnp.bfloat16)
    groups = group_scales.shape[1]
    quantized = (codes.reshape(D, groups, GROUP).astype(jnp.float32) * group_scales[:, :, None]).reshape(D, D)
    residual = (weight_tile.astype(jnp.float32) - quantized).astype(jnp.bfloat16)
    hr_value = jnp.dot(hessian, right_factor.astype(jnp.float32), precision=lax.Precision.HIGHEST)
    hr_rounded = hr_value.astype(jnp.bfloat16)
    residual_product = jnp.dot(residual, hr_rounded, preferred_element_type=jnp.float32)
    gram = lax.dot_general(right_factor, hr_rounded, (((0,), (0,)), ((), ())), preferred_element_type=jnp.float32)
    return residual_product, gram, hessian_tiles
```

```python
import functools

import jax
import jax.numpy as jnp
from jax import lax
from jax.experimental import pallas as pl
from jax.experimental.pallas import tpu as pltpu
from jax.sharding import PartitionSpec as P

CHUNKS = 4
MIB = 1024 * 1024
BF16 = jnp.bfloat16
F32 = jnp.float32


def flip(value, axis, mask):
    count = lax.axis_size(axis)
    return lax.ppermute(value, axis, [(i, i ^ mask) for i in range(count)])


def split_float(value):
    high = value.astype(BF16)
    low = (value - high.astype(F32)).astype(BF16)
    return high, low


def gather_kernel(scale, pieces, where_ref, y_ref, *refs):
    piece_refs = refs[:pieces]
    cols_ref, hr_ref, gram_ref, order_ref, sems = refs[pieces:]
    tokens = y_ref.shape[1]
    halves = pieces // y_ref.shape[0]
    width = piece_refs[0].shape[1]
    me = where_ref[0]
    copies = []
    for half in range(halves):
        for mask in range(y_ref.shape[0]):
            at = pl.multiple_of((me ^ mask) * tokens, tokens)
            index = half * y_ref.shape[0] + mask
            copy = pltpu.make_async_copy(
                piece_refs[index],
                cols_ref.at[pl.ds(at, tokens), pl.ds(half * width, width)],
                sems.at[index],
            )
            copy.start()
            copies.append(copy)
    for mask in range(y_ref.shape[0]):
        at = pl.multiple_of((me ^ mask) * tokens, tokens)
        order_ref[pl.ds(at, tokens), :] = y_ref[mask]
    y_high, y_low = split_float(order_ref[...].T)
    across = (((1,), (1,)), ((), ()))
    gram = lax.dot_general(y_high, y_high, across, preferred_element_type=F32)
    gram += lax.dot_general(y_high, y_low, across, preferred_element_type=F32)
    gram += lax.dot_general(y_low, y_high, across, preferred_element_type=F32)
    gram_ref[...] = gram * scale
    for copy in copies:
        copy.wait()
    step = min(512, cols_ref.shape[1])
    for start in range(0, cols_ref.shape[1], step):
        block = cols_ref[:, start : start + step]
        total = jnp.dot(y_high, block, preferred_element_type=F32)
        total += jnp.dot(y_low, block, preferred_element_type=F32)
        hr_ref[:, start : start + step] = (total * scale).astype(BF16)


def gather_columns(pieces, y_blocks, where, scale):
    count, tokens, rank = y_blocks.shape
    halves = len(pieces) // count
    features = halves * pieces[0].shape[1]
    return pl.pallas_call(
        functools.partial(gather_kernel, scale, len(pieces)),
        out_shape=(
            jax.ShapeDtypeStruct((count * tokens, features), BF16),
            jax.ShapeDtypeStruct((rank, features), BF16),
            jax.ShapeDtypeStruct((rank, rank), F32),
        ),
        in_specs=[
            pl.BlockSpec(memory_space=pltpu.SMEM),
            pl.BlockSpec(memory_space=pltpu.VMEM),
        ]
        + [pl.BlockSpec(memory_space=pl.ANY)] * len(pieces),
        out_specs=(pl.BlockSpec(memory_space=pltpu.VMEM),) * 3,
        scratch_shapes=[
            pltpu.VMEM((count * tokens, rank), F32),
            pltpu.SemaphoreType.DMA((len(pieces),)),
        ],
        compiler_params=pltpu.CompilerParams(vmem_limit_bytes=48 * MIB),
        name="columns_hr_gram",
    )(where, y_blocks, *pieces)


def residual_kernel(weight_ref, codes_ref, scales_ref, hr_ref, out_ref):
    groups = scales_ref.shape[1]
    width = weight_ref.shape[1] // groups
    scales = scales_ref[...]
    parts = []
    for group in range(groups):
        at = slice(group * width, (group + 1) * width)
        quantized = codes_ref[:, at].astype(F32) * scales[:, group : group + 1]
        parts.append((weight_ref[:, at].astype(F32) - quantized).astype(BF16))
    residual = jnp.concatenate(parts, axis=1)
    out_ref[...] = lax.dot_general(
        residual, hr_ref[...], (((1,), (1,)), ((), ())), preferred_element_type=F32
    ).astype(BF16)


def residual_partial(weight, codes, scales, hr):
    rows, features = weight.shape
    rank = hr.shape[0]
    block = min(256, rows)
    return pl.pallas_call(
        residual_kernel,
        out_shape=jax.ShapeDtypeStruct((rows, rank), BF16),
        grid=(rows // block,),
        in_specs=[
            pl.BlockSpec((block, features), lambda i: (i, 0)),
            pl.BlockSpec((block, features), lambda i: (i, 0)),
            pl.BlockSpec((block, scales.shape[1]), lambda i: (i, 0)),
            pl.BlockSpec((rank, features), lambda i: (0, 0)),
        ],
        out_specs=pl.BlockSpec((block, rank), lambda i: (i, 0)),
        compiler_params=pltpu.CompilerParams(vmem_limit_bytes=48 * MIB),
        name="residual_product",
    )(weight, codes, scales, hr)


def hessian_kernel(scale, rows_ref, cols_ref, *refs):
    out_ref, turned_ref = refs[-2:]

    @pl.when(pl.program_id(0) == 0)
    def _():
        turned_ref[...] = rows_ref[...].T

    total = jnp.dot(turned_ref[...], cols_ref[...], preferred_element_type=F32)
    out_ref[...] = (total * scale).astype(BF16)


def hessian_rows(rows, cols, earlier, index, shape, scale):
    tokens, height = rows.shape
    tile = min(1024, cols.shape[1])
    ins = [rows, cols]
    specs = [
        pl.BlockSpec((tokens, height), lambda j: (0, 0)),
        pl.BlockSpec((tokens, tile), lambda j: (0, j)),
    ]
    aliases = {}
    if earlier is not None:
        ins.append(earlier)
        specs.append(pl.BlockSpec(memory_space=pl.ANY))
        aliases = {2: 0}
    return pl.pallas_call(
        functools.partial(hessian_kernel, scale),
        out_shape=jax.ShapeDtypeStruct(shape, BF16),
        grid=(cols.shape[1] // tile,),
        in_specs=specs,
        out_specs=pl.BlockSpec((height, tile), lambda j: (index, j)),
        scratch_shapes=[pltpu.VMEM((height, tokens), BF16)],
        input_output_aliases=aliases,
        compiler_params=pltpu.CompilerParams(vmem_limit_bytes=48 * MIB),
        name="hessian_rows",
    )(*ins)


def body(activations, weight_tile, codes, group_scales, right_factor):
    wide_count = lax.axis_size("wide")
    narrow_count = lax.axis_size("narrow")
    wide_index = lax.axis_index("wide")
    narrow_index = lax.axis_index("narrow")
    tokens, features = activations.shape
    rows = weight_tile.shape[0]
    rank = right_factor.shape[1]
    split = features // rows
    scale = 1.0 / (tokens * wide_count)
    bits = [1 << b for b in range(1, wide_count.bit_length() - 1)]

    right_block = lax.dynamic_slice_in_dim(right_factor, narrow_index * features, features, 0)
    product = jnp.dot(activations, right_block, preferred_element_type=F32)
    mask = 1
    while mask < narrow_count:
        product = product + flip(product, "narrow", mask)
        mask *= 2
    y_blocks = product[None]
    mask = 1
    while mask < wide_count:
        y_blocks = jnp.concatenate([y_blocks, flip(y_blocks, "wide", mask)], axis=0)
        mask *= 2

    middle = features // 2
    pieces = []
    for half, order in enumerate((bits[::-1], bits)):
        held = {0: activations[:, half * middle : (half + 1) * middle]}
        for bit in order + [1]:
            held.update({m | bit: flip(held[m], "wide", bit) for m in list(held)})
        pieces += [held[m] for m in range(wide_count)]

    height = rows // CHUNKS
    row_chunks = []
    for chunk in range(CHUNKS):
        mine = jnp.stack(
            [
                activations[:, s * rows + chunk * height : s * rows + (chunk + 1) * height]
                for s in range(split)
            ]
        )
        every = lax.all_gather(mine, "narrow", axis=0, tiled=True)
        chunk_rows = lax.all_to_all(every, "wide", split_axis=0, concat_axis=0, tiled=True)
        row_chunks.append(chunk_rows.reshape(tokens * wide_count, height))

    where = wide_index.astype(jnp.int32).reshape(1)
    cols, hr, gram = gather_columns(pieces, y_blocks, where, scale)
    partial_product = residual_partial(weight_tile, codes, group_scales, hr)
    shares = partial_product.reshape(narrow_count, rows // narrow_count, rank)
    shares = lax.all_to_all(shares, "narrow", split_axis=0, concat_axis=0, tiled=True)
    residual_product = jnp.sum(shares.astype(F32), axis=0)

    hessian = None
    for chunk in range(CHUNKS):
        hessian = hessian_rows(row_chunks[chunk], cols, hessian, chunk, (rows, features), scale)
    return residual_product, gram, hessian


def solution(mesh):
    in_specs = (
        P("wide", "narrow"),
        P("wide", "narrow"),
        P("wide", "narrow"),
        P("wide", "narrow"),
        P(),
    )
    out_specs = (P(("wide", "narrow"), None), P(), P("wide", "narrow"))
    return jax.shard_map(body, mesh=mesh, in_specs=in_specs, out_specs=out_specs, check_vma=False)
```

```python
import functools

import jax
import jax.numpy as jnp
from jax import lax
from jax.experimental import pallas as pl
from jax.experimental.pallas import tpu as pltpu
from jax.sharding import PartitionSpec as P

CHUNKS = 4
PARTS = 4
MIB = 1024 * 1024
BF16 = jnp.bfloat16
F32 = jnp.float32


def flip(value, axis, mask):
    count = lax.axis_size(axis)
    return lax.ppermute(value, axis, [(i, i ^ mask) for i in range(count)])


def split_float(value):
    high = value.astype(BF16)
    low = (value - high.astype(F32)).astype(BF16)
    return high, low


def hr_kernel(scale, where_ref, cols_ref, y_ref, hr_ref, gram_ref, order_ref, high_ref, low_ref):
    @pl.when(pl.program_id(0) == 0)
    def _():
        count, tokens = y_ref.shape[:2]
        for mask in range(count):
            at = pl.multiple_of((where_ref[0] ^ mask) * tokens, tokens)
            order_ref[pl.ds(at, tokens), :] = y_ref[mask]
        y_high, y_low = split_float(order_ref[...].T)
        high_ref[...] = y_high
        low_ref[...] = y_low
        across = (((1,), (1,)), ((), ()))
        gram = lax.dot_general(y_high, y_high, across, preferred_element_type=F32)
        gram += lax.dot_general(y_high, y_low, across, preferred_element_type=F32)
        gram += lax.dot_general(y_low, y_high, across, preferred_element_type=F32)
        gram_ref[...] = gram * scale

    total = jnp.dot(high_ref[...], cols_ref[...], preferred_element_type=F32)
    total += jnp.dot(low_ref[...], cols_ref[...], preferred_element_type=F32)
    hr_ref[...] = (total * scale).astype(BF16)


def hr_and_gram(cols, y_blocks, where, scale):
    tokens, features = cols.shape
    rank = y_blocks.shape[2]
    tile = min(512, features)
    return pl.pallas_call(
        functools.partial(hr_kernel, scale),
        out_shape=(
            jax.ShapeDtypeStruct((rank, features), BF16),
            jax.ShapeDtypeStruct((rank, rank), F32),
        ),
        grid=(features // tile,),
        in_specs=[
            pl.BlockSpec(memory_space=pltpu.SMEM),
            pl.BlockSpec((tokens, tile), lambda j: (0, j)),
            pl.BlockSpec(y_blocks.shape, lambda j: (0, 0, 0)),
        ],
        out_specs=(
            pl.BlockSpec((rank, tile), lambda j: (0, j)),
            pl.BlockSpec((rank, rank), lambda j: (0, 0)),
        ),
        scratch_shapes=[
            pltpu.VMEM((tokens, rank), F32),
            pltpu.VMEM((rank, tokens), BF16),
            pltpu.VMEM((rank, tokens), BF16),
        ],
        compiler_params=pltpu.CompilerParams(vmem_limit_bytes=48 * MIB),
        name="hr_and_gram",
    )(where, cols, y_blocks)


def place_kernel(count, sources, where_ref, *refs):
    out_ref, sems = refs[-2:]
    me = where_ref[0]
    half = count // 2
    waits = []
    for mask in range(count):
        other = me ^ mask
        near, far = sources[mask]
        target = out_ref.at[other]

        def start(index, target=target, mask=mask):
            pltpu.make_async_copy(refs[index], target, sems.at[mask]).start()

        if far is None:
            start(near)
        elif near is None:
            start(far)
        else:
            close = jnp.abs(me - other) <= half
            pl.when(close)(functools.partial(start, near))
            pl.when(jnp.logical_not(close))(functools.partial(start, far))
        some = far if near is None else near
        waits.append(pltpu.make_async_copy(refs[some], target, sems.at[mask]))
    for wait in waits:
        wait.wait()


def place_blocks(blocks, sources, where, after):
    count = len(sources)
    return pl.pallas_call(
        functools.partial(place_kernel, count, sources),
        out_shape=jax.ShapeDtypeStruct((count,) + blocks[0].shape, BF16),
        in_specs=[pl.BlockSpec(memory_space=pltpu.SMEM)]
        + [pl.BlockSpec(memory_space=pl.ANY)] * (len(blocks) + len(after)),
        out_specs=pl.BlockSpec(memory_space=pl.ANY),
        scratch_shapes=[pltpu.SemaphoreType.DMA((count,))],
        name="place_blocks",
    )(where, *blocks, *after)


def exchange_blocks(mine):
    count = lax.axis_size("narrow")
    half = count // 2
    blocks = [mine]
    sources = [(0, None)]
    direct = {}
    order = sorted(range(1, count), key=lambda m: (m != half, m))
    for mask in order:
        pairs = [(i, i ^ mask) for i in range(count) if abs(i - (i ^ mask)) <= half]
        direct[mask] = lax.ppermute(mine, "narrow", pairs) if pairs else None
    for mask in range(1, count):
        near = far = None
        if direct[mask] is not None:
            near = len(blocks)
            blocks.append(direct[mask])
        pairs = [(i ^ half, i ^ mask) for i in range(count) if abs(i - (i ^ mask)) > half]
        if pairs:
            far = len(blocks)
            blocks.append(lax.ppermute(direct[half], "narrow", pairs))
        sources.append((near, far))
    return blocks, sources


def residual_kernel(weight_ref, codes_ref, scales_ref, *refs):
    out_ref = refs[-1]
    groups = scales_ref.shape[1]
    width = weight_ref.shape[1] // groups
    scales = scales_ref[...]
    for group in range(groups):
        at = slice(group * width, (group + 1) * width)
        quantized = codes_ref[:, at].astype(F32) * scales[:, group : group + 1]
        out_ref[:, at] = (weight_ref[:, at].astype(F32) - quantized).astype(BF16)


def residual_part(weight, codes, scales, earlier, index, count, after):
    rows, features = weight.shape
    block = min(64, rows // count)
    steps = rows // count // block
    place = lambda i: (index * steps + i, 0)
    ins = [weight, codes, scales]
    specs = [
        pl.BlockSpec((block, features), place),
        pl.BlockSpec((block, features), place),
        pl.BlockSpec((block, scales.shape[1]), place),
    ]
    aliases = {}
    if earlier is not None:
        aliases = {len(ins): 0}
        ins.append(earlier)
        specs.append(pl.BlockSpec(memory_space=pl.ANY))
    for value in after:
        ins.append(value)
        specs.append(pl.BlockSpec(memory_space=pl.ANY))
    return pl.pallas_call(
        residual_kernel,
        out_shape=jax.ShapeDtypeStruct((rows, features), BF16),
        grid=(steps,),
        in_specs=specs,
        out_specs=pl.BlockSpec((block, features), place),
        input_output_aliases=aliases,
        compiler_params=pltpu.CompilerParams(vmem_limit_bytes=48 * MIB),
        name="residual_part",
    )(*ins)


def product_kernel(residual_ref, hr_ref, out_ref):
    out_ref[...] = lax.dot_general(
        residual_ref[...], hr_ref[...], (((1,), (1,)), ((), ())), preferred_element_type=F32
    ).astype(BF16)


def partial_product(residual, hr):
    rows, features = residual.shape
    rank = hr.shape[0]
    block = min(256, rows)
    return pl.pallas_call(
        product_kernel,
        out_shape=jax.ShapeDtypeStruct((rows, rank), BF16),
        grid=(rows // block,),
        in_specs=[
            pl.BlockSpec((block, features), lambda i: (i, 0)),
            pl.BlockSpec((rank, features), lambda i: (0, 0)),
        ],
        out_specs=pl.BlockSpec((block, rank), lambda i: (i, 0)),
        compiler_params=pltpu.CompilerParams(vmem_limit_bytes=48 * MIB),
        name="partial_product",
    )(residual, hr)


def hessian_kernel(scale, rows_ref, cols_ref, *refs):
    out_ref, turned_ref = refs[-2:]

    @pl.when(pl.program_id(0) == 0)
    def _():
        turned_ref[...] = rows_ref[...].T

    total = jnp.dot(turned_ref[...], cols_ref[...], preferred_element_type=F32)
    out_ref[...] = (total * scale).astype(BF16)


def hessian_rows(rows, cols, earlier, index, shape, scale):
    tokens, height = rows.shape
    tile = min(1024, cols.shape[1])
    ins = [rows, cols]
    specs = [
        pl.BlockSpec((tokens, height), lambda j: (0, 0)),
        pl.BlockSpec((tokens, tile), lambda j: (0, j)),
    ]
    aliases = {}
    if earlier is not None:
        ins.append(earlier)
        specs.append(pl.BlockSpec(memory_space=pl.ANY))
        aliases = {2: 0}
    return pl.pallas_call(
        functools.partial(hessian_kernel, scale),
        out_shape=jax.ShapeDtypeStruct(shape, BF16),
        grid=(cols.shape[1] // tile,),
        in_specs=specs,
        out_specs=pl.BlockSpec((height, tile), lambda j: (index, j)),
        scratch_shapes=[pltpu.VMEM((height, tokens), BF16)],
        input_output_aliases=aliases,
        compiler_params=pltpu.CompilerParams(vmem_limit_bytes=48 * MIB),
        name="hessian_rows",
    )(*ins)


def body(activations, weight_tile, codes, group_scales, right_factor):
    wide_count = lax.axis_size("wide")
    narrow_count = lax.axis_size("narrow")
    narrow_index = lax.axis_index("narrow")
    tokens, features = activations.shape
    rows = weight_tile.shape[0]
    rank = right_factor.shape[1]
    split = features // rows
    scale = 1.0 / (tokens * wide_count)

    cols = lax.all_gather(activations, "wide", axis=0, tiled=True)

    height = rows // CHUNKS
    chunks = []
    for chunk in range(CHUNKS):
        mine = jnp.stack(
            [
                activations[:, s * rows + chunk * height : s * rows + (chunk + 1) * height]
                for s in range(split)
            ]
        )
        chunks.append(exchange_blocks(mine))

    right_block = lax.dynamic_slice_in_dim(right_factor, narrow_index * features, features, 0)
    product = jnp.dot(activations, right_block, preferred_element_type=F32)
    mask = 1
    while mask < narrow_count:
        product = product + flip(product, "narrow", mask)
        mask *= 2
    y_blocks = product[None]
    mask = 1
    while mask < wide_count:
        y_blocks = jnp.concatenate([y_blocks, flip(y_blocks, "wide", mask)], axis=0)
        mask *= 2

    residual = None
    for part in range(PARTS):
        residual = residual_part(
            weight_tile, codes, group_scales, residual, part, PARTS, [product] if part == 1 else []
        )

    where = narrow_index.astype(jnp.int32).reshape(1)
    row_chunks = []
    for chunk in range(CHUNKS):
        blocks, sources = chunks[chunk]
        after = [residual] if chunk == 0 else []
        every = place_blocks(blocks, sources, where, after)
        every = every.reshape(narrow_count * split, tokens, height)
        chunk_rows = lax.all_to_all(every, "wide", split_axis=0, concat_axis=0, tiled=True)
        row_chunks.append(chunk_rows.reshape(tokens * wide_count, height))

    hr, gram = hr_and_gram(cols, y_blocks, lax.axis_index("wide").astype(jnp.int32).reshape(1), scale)
    shares = partial_product(residual, hr)
    shares = shares.reshape(narrow_count, rows // narrow_count, rank)
    shares = lax.all_to_all(shares, "narrow", split_axis=0, concat_axis=0, tiled=True)
    residual_product = jnp.sum(shares.astype(F32), axis=0)

    hessian = None
    for chunk in range(CHUNKS):
        hessian = hessian_rows(row_chunks[chunk], cols, hessian, chunk, (rows, features), scale)
    return residual_product, gram, hessian


def solution(mesh):
    in_specs = (
        P("wide", "narrow"),
        P("wide", "narrow"),
        P("wide", "narrow"),
        P("wide", "narrow"),
        P(),
    )
    out_specs = (P(("wide", "narrow"), None), P(), P("wide", "narrow"))
    return jax.shard_map(body, mesh=mesh, in_specs=in_specs, out_specs=out_specs, check_vma=False)
```

```python
import functools

import jax
import jax.numpy as jnp
from jax import lax
from jax.experimental import pallas as pl
from jax.experimental.pallas import tpu as pltpu
from jax.sharding import PartitionSpec as P

CHUNKS = 4
PARTS = 4
MIB = 1024 * 1024
BF16 = jnp.bfloat16
F32 = jnp.float32


def flip(value, axis, mask):
    count = lax.axis_size(axis)
    return lax.ppermute(value, axis, [(i, i ^ mask) for i in range(count)])


def split_float(value):
    high = value.astype(BF16)
    low = (value - high.astype(F32)).astype(BF16)
    return high, low


def hr_kernel(scale, where_ref, cols_ref, y_ref, hr_ref, gram_ref, order_ref, both_ref):
    rank = hr_ref.shape[1]

    @pl.when(pl.program_id(0) == 0)
    def _():
        count, tokens = y_ref.shape[:2]
        for mask in range(count):
            at = pl.multiple_of((where_ref[0] ^ mask) * tokens, tokens)
            order_ref[pl.ds(at, tokens), :] = y_ref[mask]
        y_high, y_low = split_float(order_ref[...].T)
        both_ref[:rank] = y_high
        both_ref[rank:] = y_low
        across = (((1,), (1,)), ((), ()))
        gram = lax.dot_general(both_ref[...], y_high, across, preferred_element_type=F32)
        cross = gram[rank:]
        gram_ref[...] = (gram[:rank] + (cross + cross.T)) * scale

    total = jnp.dot(both_ref[...], cols_ref[...], preferred_element_type=F32)
    hr_ref[...] = ((total[:rank] + total[rank:]) * scale).T.astype(BF16)


def hr_and_gram(cols, y_blocks, where, scale, after):
    tokens, features = cols.shape
    rank = y_blocks.shape[2]
    tile = min(1024, features)

    def kernel(*refs):
        hr_kernel(scale, *refs[:3], *refs[3 + len(after) :])

    return pl.pallas_call(
        kernel,
        out_shape=(
            jax.ShapeDtypeStruct((features, rank), BF16),
            jax.ShapeDtypeStruct((rank, rank), F32),
        ),
        grid=(features // tile,),
        in_specs=[
            pl.BlockSpec(memory_space=pltpu.SMEM),
            pl.BlockSpec((tokens, tile), lambda j: (0, j)),
            pl.BlockSpec(y_blocks.shape, lambda j: (0, 0, 0)),
        ]
        + [pl.BlockSpec(memory_space=pl.ANY)] * len(after),
        out_specs=(
            pl.BlockSpec((tile, rank), lambda j: (j, 0)),
            pl.BlockSpec((rank, rank), lambda j: (0, 0)),
        ),
        scratch_shapes=[
            pltpu.VMEM((tokens, rank), F32),
            pltpu.VMEM((2 * rank, tokens), BF16),
        ],
        compiler_params=pltpu.CompilerParams(vmem_limit_bytes=48 * MIB),
        name="hr_and_gram",
    )(where, cols, y_blocks, *after)


def place_kernel(sources, where_ref, *refs):
    out_ref = refs[-1]
    count = len(sources)
    me = where_ref[0]
    for mask in range(count):
        other = me ^ mask
        near, far = sources[mask]

        def put(index, other=other):
            out_ref[other] = refs[index][...]

        if far is None:
            put(near)
        elif near is None:
            put(far)
        else:
            close = jnp.abs(me - other) <= count // 2
            pl.when(close)(functools.partial(put, near))
            pl.when(jnp.logical_not(close))(functools.partial(put, far))


def place_blocks(blocks, sources, where, after):
    count = len(sources)
    return pl.pallas_call(
        functools.partial(place_kernel, sources),
        out_shape=jax.ShapeDtypeStruct((count,) + blocks[0].shape, BF16),
        in_specs=[pl.BlockSpec(memory_space=pltpu.SMEM)]
        + [pl.BlockSpec(memory_space=pltpu.VMEM)] * len(blocks)
        + [pl.BlockSpec(memory_space=pl.ANY)] * len(after),
        out_specs=pl.BlockSpec(memory_space=pltpu.VMEM),
        compiler_params=pltpu.CompilerParams(vmem_limit_bytes=48 * MIB),
        name="place_blocks",
    )(where, *blocks, *after)


def exchange_blocks(mine):
    count = lax.axis_size("narrow")
    half = count // 2
    blocks = [mine]
    sources = [(0, None)]
    direct = {}
    order = sorted(range(1, count), key=lambda m: (m != half, m))
    for mask in order:
        pairs = [(i, i ^ mask) for i in range(count) if abs(i - (i ^ mask)) <= half]
        direct[mask] = lax.ppermute(mine, "narrow", pairs) if pairs else None
    for mask in range(1, count):
        near = far = None
        if direct[mask] is not None:
            near = len(blocks)
            blocks.append(direct[mask])
        pairs = [(i ^ half, i ^ mask) for i in range(count) if abs(i - (i ^ mask)) > half]
        if pairs:
            far = len(blocks)
            blocks.append(lax.ppermute(direct[half], "narrow", pairs))
        sources.append((near, far))
    return blocks, sources


def residual_kernel(weight_ref, codes_ref, scales_ref, *refs):
    out_ref = refs[-1]
    groups = scales_ref.shape[1]
    width = weight_ref.shape[1] // groups
    scales = scales_ref[...]
    batch = min(8, groups)
    for first in range(0, groups, batch):
        parts = []
        for group in range(first, first + batch):
            at = slice(group * width, (group + 1) * width)
            quantized = codes_ref[:, at].astype(F32) * scales[:, group : group + 1]
            parts.append((weight_ref[:, at].astype(F32) - quantized).astype(BF16))
        out_ref[:, first * width : (first + batch) * width] = jnp.concatenate(parts, axis=1)


def residual_part(weight, codes, scales, earlier, index, count, after):
    rows, features = weight.shape
    block = min(128, rows // count)
    steps = rows // count // block
    place = lambda i: (index * steps + i, 0)
    ins = [weight, codes, scales]
    specs = [
        pl.BlockSpec((block, features), place),
        pl.BlockSpec((block, features), place),
        pl.BlockSpec((block, scales.shape[1]), place),
    ]
    aliases = {}
    if earlier is not None:
        aliases = {len(ins): 0}
        ins.append(earlier)
        specs.append(pl.BlockSpec(memory_space=pl.ANY))
    for value in after:
        ins.append(value)
        specs.append(pl.BlockSpec(memory_space=pl.ANY))
    return pl.pallas_call(
        residual_kernel,
        out_shape=jax.ShapeDtypeStruct((rows, features), BF16),
        grid=(steps,),
        in_specs=specs,
        out_specs=pl.BlockSpec((block, features), place),
        input_output_aliases=aliases,
        compiler_params=pltpu.CompilerParams(vmem_limit_bytes=48 * MIB),
        name="residual_part",
    )(*ins)


def product_kernel(residual_ref, hr_ref, out_ref):
    out_ref[...] = jnp.dot(residual_ref[...], hr_ref[...], preferred_element_type=F32).astype(BF16)


def partial_product(residual, hr):
    rows, features = residual.shape
    rank = hr.shape[1]
    block = min(512, rows)
    return pl.pallas_call(
        product_kernel,
        out_shape=jax.ShapeDtypeStruct((rows, rank), BF16),
        grid=(rows // block,),
        in_specs=[
            pl.BlockSpec((block, features), lambda i: (i, 0)),
            pl.BlockSpec((features, rank), lambda i: (0, 0)),
        ],
        out_specs=pl.BlockSpec((block, rank), lambda i: (i, 0)),
        compiler_params=pltpu.CompilerParams(vmem_limit_bytes=48 * MIB),
        name="partial_product",
    )(residual, hr)


def hessian_rows(row_chunks, cols, earlier, index, shape, scale, after):
    tokens, height = row_chunks[0].shape
    block = height * len(row_chunks)
    tile = min(512, cols.shape[1])
    count = len(row_chunks)
    ins = [*row_chunks, cols]
    specs = [pl.BlockSpec((tokens, height), lambda j: (0, 0))] * count
    specs.append(pl.BlockSpec((tokens, tile), lambda j: (0, j)))
    aliases = {}
    if earlier is not None:
        aliases = {len(ins): 0}
        ins.append(earlier)
        specs.append(pl.BlockSpec(memory_space=pl.ANY))
    for value in after:
        ins.append(value)
        specs.append(pl.BlockSpec(memory_space=pl.ANY))

    def kernel(*refs):
        cols_ref = refs[count]
        out_ref, turned_ref = refs[-2:]

        @pl.when(pl.program_id(0) == 0)
        def _():
            for chunk in range(count):
                turned_ref[chunk * height : (chunk + 1) * height] = refs[chunk][...].T

        total = jnp.dot(turned_ref[...], cols_ref[...], preferred_element_type=F32)
        out_ref[...] = (total * scale).astype(BF16)

    return pl.pallas_call(
        kernel,
        out_shape=jax.ShapeDtypeStruct(shape, BF16),
        grid=(cols.shape[1] // tile,),
        in_specs=specs,
        out_specs=pl.BlockSpec((block, tile), lambda j: (index, j)),
        scratch_shapes=[pltpu.VMEM((block, tokens), BF16)],
        input_output_aliases=aliases,
        compiler_params=pltpu.CompilerParams(vmem_limit_bytes=48 * MIB),
        name="hessian_rows",
    )(*ins)


def body(activations, weight_tile, codes, group_scales, right_factor):
    wide_count = lax.axis_size("wide")
    narrow_count = lax.axis_size("narrow")
    narrow_index = lax.axis_index("narrow")
    tokens, features = activations.shape
    rows = weight_tile.shape[0]
    rank = right_factor.shape[1]
    split = features // rows
    scale = 1.0 / (tokens * wide_count)

    cols = lax.all_gather(activations, "wide", axis=0, tiled=True)

    height = rows // CHUNKS
    chunks = []
    for chunk in range(CHUNKS):
        mine = jnp.stack(
            [
                activations[:, s * rows + chunk * height : s * rows + (chunk + 1) * height]
                for s in range(split)
            ]
        )
        chunks.append(exchange_blocks(mine))

    right_block = lax.dynamic_slice_in_dim(right_factor, narrow_index * features, features, 0)
    product = jnp.dot(activations, right_block, preferred_element_type=F32)
    steps = []
    mask = 1
    while mask < narrow_count:
        product = product + flip(product, "narrow", mask)
        steps.append(product)
        mask *= 2
    y_blocks = product[None]
    mask = 1
    while mask < wide_count:
        y_blocks = jnp.concatenate([y_blocks, flip(y_blocks, "wide", mask)], axis=0)
        steps.append(y_blocks)
        mask *= 2

    residual = None
    for part in range(PARTS):
        after = steps[part - 1 : part] if part else []
        residual = residual_part(
            weight_tile, codes, group_scales, residual, part, PARTS, after
        )

    where = narrow_index.astype(jnp.int32).reshape(1)
    row_chunks = []
    placed = []
    for chunk in range(CHUNKS):
        blocks, sources = chunks[chunk]
        after = placed[-1:] if chunk else [residual]
        if chunk + 1 < CHUNKS:
            after = after + [chunks[chunk + 1][0][1]]
        every = place_blocks(blocks, sources, where, after)
        placed.append(every)
        every = every.reshape(narrow_count * split, tokens, height)
        chunk_rows = lax.all_to_all(every, "wide", split_axis=0, concat_axis=0, tiled=True)
        row_chunks.append(chunk_rows.reshape(tokens * wide_count, height))

    wide_where = lax.axis_index("wide").astype(jnp.int32).reshape(1)
    hr, gram = hr_and_gram(cols, y_blocks, wide_where, scale, placed[2:3])
    partial = partial_product(residual, hr)
    shares = partial.reshape(narrow_count, rows // narrow_count, rank)
    shares = lax.all_to_all(shares, "narrow", split_axis=0, concat_axis=0, tiled=True)
    residual_product = jnp.sum(shares.astype(F32), axis=0)

    shape = (rows, features)
    hessian = hessian_rows(row_chunks[:-1], cols, None, 0, shape, scale, [placed[-1], partial])
    hessian = hessian_rows(row_chunks[-1:], cols, hessian, CHUNKS - 1, shape, scale, [])
    return residual_product, gram, hessian


def solution(mesh):
    in_specs = (
        P("wide", "narrow"),
        P("wide", "narrow"),
        P("wide", "narrow"),
        P("wide", "narrow"),
        P(),
    )
    out_specs = (P(("wide", "narrow"), None), P(), P("wide", "narrow"))
    return jax.shard_map(body, mesh=mesh, in_specs=in_specs, out_specs=out_specs, check_vma=False)
```

```python
import functools

import jax
import jax.numpy as jnp
from jax import lax
from jax.experimental import pallas as pl
from jax.experimental.pallas import tpu as pltpu
from jax.sharding import PartitionSpec as P

CHUNKS = 2
MIB = 1024 * 1024
BF16 = jnp.bfloat16
F32 = jnp.float32


def flip(value, axis, mask):
    count = lax.axis_size(axis)
    return lax.ppermute(value, axis, [(i, i ^ mask) for i in range(count)])


def split_float(value):
    high = value.astype(BF16)
    low = (value - high.astype(F32)).astype(BF16)
    return high, low


def hr_and_gram(cols, y_blocks, where, scale, after):
    count = len(y_blocks)
    tokens, rank = y_blocks[0].shape
    features = cols.shape[1]
    tile = min(1024, features)

    def kernel(where_ref, cols_ref, *refs):
        hr_ref, gram_ref, order_ref, both_ref = refs[-4:]

        @pl.when(pl.program_id(0) == 0)
        def _():
            for mask in range(count):
                at = pl.multiple_of((where_ref[0] ^ mask) * tokens, tokens)
                order_ref[pl.ds(at, tokens), :] = refs[mask][...]
            y_high, y_low = split_float(order_ref[...].T)
            both_ref[:rank] = y_high
            both_ref[rank:] = y_low
            across = (((1,), (1,)), ((), ()))
            gram = lax.dot_general(both_ref[...], y_high, across, preferred_element_type=F32)
            cross = gram[rank:]
            gram_ref[...] = (gram[:rank] + (cross + cross.T)) * scale

        total = jnp.dot(both_ref[...], cols_ref[...], preferred_element_type=F32)
        hr_ref[...] = ((total[:rank] + total[rank:]) * scale).T.astype(BF16)

    return pl.pallas_call(
        kernel,
        out_shape=(
            jax.ShapeDtypeStruct((features, rank), BF16),
            jax.ShapeDtypeStruct((rank, rank), F32),
        ),
        grid=(features // tile,),
        in_specs=[
            pl.BlockSpec(memory_space=pltpu.SMEM),
            pl.BlockSpec((count * tokens, tile), lambda j: (0, j)),
        ]
        + [pl.BlockSpec((tokens, rank), lambda j: (0, 0))] * count
        + [pl.BlockSpec(memory_space=pl.ANY)] * len(after),
        out_specs=(
            pl.BlockSpec((tile, rank), lambda j: (j, 0)),
            pl.BlockSpec((rank, rank), lambda j: (0, 0)),
        ),
        scratch_shapes=[
            pltpu.VMEM((count * tokens, rank), F32),
            pltpu.VMEM((2 * rank, count * tokens), BF16),
        ],
        compiler_params=pltpu.CompilerParams(vmem_limit_bytes=48 * MIB),
        name="hr_and_gram",
    )(where, cols, *y_blocks, *after)


def residual_kernel(weight_ref, codes_ref, scales_ref, out_ref):
    groups = scales_ref.shape[1]
    width = weight_ref.shape[1] // groups
    scales = scales_ref[...]
    parts = []
    for group in range(groups):
        at = slice(group * width, (group + 1) * width)
        quantized = codes_ref[:, at].astype(F32) * scales[:, group : group + 1]
        parts.append((weight_ref[:, at].astype(F32) - quantized).astype(BF16))
    out_ref[...] = jnp.concatenate(parts, axis=1)


def residual_tile(weight, codes, scales):
    rows, features = weight.shape
    block = min(256, rows)
    return pl.pallas_call(
        residual_kernel,
        out_shape=jax.ShapeDtypeStruct((rows, features), BF16),
        grid=(rows // block,),
        in_specs=[
            pl.BlockSpec((block, features), lambda i: (i, 0)),
            pl.BlockSpec((block, features), lambda i: (i, 0)),
            pl.BlockSpec((block, scales.shape[1]), lambda i: (i, 0)),
        ],
        out_specs=pl.BlockSpec((block, features), lambda i: (i, 0)),
        compiler_params=pltpu.CompilerParams(vmem_limit_bytes=48 * MIB),
        name="residual_tile",
    )(weight, codes, scales)


def product_kernel(residual_ref, hr_ref, out_ref):
    out_ref[...] = jnp.dot(residual_ref[...], hr_ref[...], preferred_element_type=F32).astype(BF16)


def partial_product(residual, hr):
    rows, features = residual.shape
    rank = hr.shape[1]
    block = min(512, rows)
    return pl.pallas_call(
        product_kernel,
        out_shape=jax.ShapeDtypeStruct((rows, rank), BF16),
        grid=(rows // block,),
        in_specs=[
            pl.BlockSpec((block, features), lambda i: (i, 0)),
            pl.BlockSpec((features, rank), lambda i: (0, 0)),
        ],
        out_specs=pl.BlockSpec((block, rank), lambda i: (i, 0)),
        compiler_params=pltpu.CompilerParams(vmem_limit_bytes=48 * MIB),
        name="partial_product",
    )(residual, hr)


def hessian_rows(pieces, first, cols, earlier, index, shape, scale, after):
    tokens, block = pieces[0].shape
    count = len(pieces)
    tile = min(512, cols.shape[1])
    ins = [first, *pieces, cols]
    specs = [pl.BlockSpec(memory_space=pltpu.SMEM)]
    specs += [pl.BlockSpec((tokens, block), lambda j: (0, 0))] * count
    specs.append(pl.BlockSpec((count * tokens, tile), lambda j: (0, j)))
    aliases = {}
    if earlier is not None:
        aliases = {len(ins): 0}
        ins.append(earlier)
        specs.append(pl.BlockSpec(memory_space=pl.ANY))
    for value in after:
        ins.append(value)
        specs.append(pl.BlockSpec(memory_space=pl.ANY))

    def kernel(first_ref, *refs):
        cols_ref = refs[count]
        out_ref, rows_ref, turned_ref = refs[-3:]

        @pl.when(pl.program_id(0) == 0)
        def _():
            for k in range(count):
                at = pl.multiple_of((first_ref[0] ^ k) * tokens, tokens)
                rows_ref[pl.ds(at, tokens), :] = refs[k][...]
            turned_ref[...] = rows_ref[...].T

        total = jnp.dot(turned_ref[...], cols_ref[...], preferred_element_type=F32)
        out_ref[...] = (total * scale).astype(BF16)

    return pl.pallas_call(
        kernel,
        out_shape=jax.ShapeDtypeStruct(shape, BF16),
        grid=(cols.shape[1] // tile,),
        in_specs=specs,
        out_specs=pl.BlockSpec((block, tile), lambda j: (index, j)),
        scratch_shapes=[
            pltpu.VMEM((count * tokens, block), BF16),
            pltpu.VMEM((block, count * tokens), BF16),
        ],
        input_output_aliases=aliases,
        compiler_params=pltpu.CompilerParams(vmem_limit_bytes=48 * MIB),
        name="hessian_rows",
    )(*ins)


def pair_sum(values):
    while len(values) > 1:
        values = [values[i] + values[i + 1] for i in range(0, len(values), 2)]
    return values[0]


def body(activations, weight_tile, codes, group_scales, right_factor):
    wide_count = lax.axis_size("wide")
    narrow_count = lax.axis_size("narrow")
    wide_index = lax.axis_index("wide")
    narrow_index = lax.axis_index("narrow")
    tokens, features = activations.shape
    rows = weight_tile.shape[0]
    split = features // rows
    scale = 1.0 / (tokens * wide_count)

    cols = lax.all_gather(activations, "wide", axis=0, tiled=True)

    right_block = lax.dynamic_slice_in_dim(right_factor, narrow_index * features, features, 0)
    product = jnp.dot(activations, right_block, preferred_element_type=F32)
    product = pair_sum([product] + [flip(product, "narrow", m) for m in range(1, narrow_count)])
    y_blocks = [product] + [flip(product, "wide", m) for m in range(1, wide_count)]

    height = rows // CHUNKS
    row_pieces = []
    for chunk in range(CHUNKS):
        operands = []
        for k in range(split):
            at = ((wide_index ^ k) % split) * rows + chunk * height
            operands.append(lax.dynamic_slice_in_dim(activations, at, height, 1))
        pieces = []
        for k in range(wide_count):
            pairs = []
            for w in range(wide_count):
                u = w ^ k
                for n in range(narrow_count):
                    target = (n * split + u % split) * narrow_count + u // split
                    pairs.append((w * narrow_count + n, target))
            pieces.append(lax.ppermute(operands[k % split], ("wide", "narrow"), pairs))
        row_pieces.append(pieces)
    first = (narrow_index * split + wide_index % split).astype(jnp.int32).reshape(1)

    residual = residual_tile(weight_tile, codes, group_scales)
    shape = (rows, features)
    hessian = hessian_rows(row_pieces[0], first, cols, None, 0, shape, scale, [residual])

    hr, gram = hr_and_gram(
        cols, y_blocks, wide_index.astype(jnp.int32).reshape(1), scale, [hessian]
    )
    partial = partial_product(residual, hr)
    share = rows // narrow_count
    received = []
    for m in range(narrow_count):
        piece = lax.dynamic_slice_in_dim(partial, (narrow_index ^ m) * share, share, 0)
        received.append(flip(piece, "narrow", m) if m else piece)
    residual_product = pair_sum([piece.astype(F32) for piece in received])

    for chunk in range(1, CHUNKS):
        hessian = hessian_rows(
            row_pieces[chunk], first, cols, hessian, chunk, shape, scale, [partial]
        )
    return residual_product, gram, hessian


def solution(mesh):
    in_specs = (
        P("wide", "narrow"),
        P("wide", "narrow"),
        P("wide", "narrow"),
        P("wide", "narrow"),
        P(),
    )
    out_specs = (P(("wide", "narrow"), None), P(), P("wide", "narrow"))
    return jax.shard_map(body, mesh=mesh, in_specs=in_specs, out_specs=out_specs, check_vma=False)
```

```python
import functools

import jax
import jax.numpy as jnp
from jax import lax
from jax.experimental import pallas as pl
from jax.experimental.pallas import tpu as pltpu
from jax.sharding import PartitionSpec as P

PARTS = (4, 2, 2)
MIB = 1024 * 1024
BF16 = jnp.bfloat16
F32 = jnp.float32


def flip(value, axis, mask):
    count = lax.axis_size(axis)
    return lax.ppermute(value, axis, [(i, i ^ mask) for i in range(count)])


def hold(value, *after):
    return pl.pallas_call(
        lambda *refs: None,
        out_shape=jax.ShapeDtypeStruct(value.shape, value.dtype),
        in_specs=[pl.BlockSpec(memory_space=pl.ANY)] * (1 + len(after)),
        out_specs=pl.BlockSpec(memory_space=pl.ANY),
        input_output_aliases={0: 0},
        name="hold",
    )(value, *after)


def columns_hr_gram(pieces, y_blocks, where, scale):
    count, tokens, rank = y_blocks.shape
    halves = len(pieces) // count
    width = pieces[0].shape[1]
    features = halves * width
    step = min(1024, width)

    def kernel(where_ref, y_ref, *refs):
        cols_ref, hr_ref, gram_ref, order_ref, sems = refs[len(pieces) :]
        me = where_ref[0]
        copies = []
        for half in range(halves):
            for mask in range(count):
                at = pl.multiple_of((me ^ mask) * tokens, tokens)
                index = half * count + mask
                copy = pltpu.make_async_copy(
                    refs[index],
                    cols_ref.at[pl.ds(at, tokens), pl.ds(half * width, width)],
                    sems.at[index],
                )
                copy.start()
                copies.append(copy)
        for mask in range(count):
            at = pl.multiple_of((me ^ mask) * tokens, tokens)
            order_ref[pl.ds(at, tokens), :] = y_ref[mask]
        turned = order_ref[...].T
        gram = jnp.dot(turned, order_ref[...], preferred_element_type=F32)
        gram_ref[...] = gram * scale
        for half in range(halves):
            for copy in copies[half * count : (half + 1) * count]:
                copy.wait()
            for start in range(half * width, (half + 1) * width, step):
                block = cols_ref[:, start : start + step]
                total = jnp.dot(turned, block, preferred_element_type=F32) * scale
                hr_ref[start : start + step, :] = total.T.astype(BF16)

    return pl.pallas_call(
        kernel,
        out_shape=(
            jax.ShapeDtypeStruct((count * tokens, features), BF16),
            jax.ShapeDtypeStruct((features, rank), BF16),
            jax.ShapeDtypeStruct((rank, rank), F32),
        ),
        in_specs=[
            pl.BlockSpec(memory_space=pltpu.SMEM),
            pl.BlockSpec(memory_space=pltpu.VMEM),
        ]
        + [pl.BlockSpec(memory_space=pl.ANY)] * len(pieces),
        out_specs=(pl.BlockSpec(memory_space=pltpu.VMEM),) * 3,
        scratch_shapes=[
            pltpu.VMEM((count * tokens, rank), BF16),
            pltpu.SemaphoreType.DMA((len(pieces),)),
        ],
        compiler_params=pltpu.CompilerParams(vmem_limit_bytes=48 * MIB),
        name="columns_hr_gram",
    )(where, y_blocks, *pieces)


def residual_kernel(weight_ref, codes_ref, scales_ref, hr_ref, after_ref, out_ref):
    groups = scales_ref.shape[1]
    width = weight_ref.shape[1] // groups
    scales = scales_ref[...]
    parts = []
    for group in range(groups):
        at = slice(group * width, (group + 1) * width)
        quantized = codes_ref[:, at].astype(F32) * scales[:, group : group + 1]
        parts.append((weight_ref[:, at].astype(F32) - quantized).astype(BF16))
    residual = jnp.concatenate(parts, axis=1)
    out_ref[...] = jnp.dot(residual, hr_ref[...], preferred_element_type=F32).astype(BF16)


def residual_partial(weight, codes, scales, hr, after):
    rows, features = weight.shape
    rank = hr.shape[1]
    block = min(256, rows)
    return pl.pallas_call(
        residual_kernel,
        out_shape=jax.ShapeDtypeStruct((rows, rank), BF16),
        grid=(rows // block,),
        in_specs=[
            pl.BlockSpec((block, features), lambda i: (i, 0)),
            pl.BlockSpec((block, features), lambda i: (i, 0)),
            pl.BlockSpec((block, scales.shape[1]), lambda i: (i, 0)),
            pl.BlockSpec((features, rank), lambda i: (0, 0)),
            pl.BlockSpec(memory_space=pl.ANY),
        ],
        out_specs=pl.BlockSpec((block, rank), lambda i: (i, 0)),
        compiler_params=pltpu.CompilerParams(vmem_limit_bytes=48 * MIB),
        name="residual_product",
    )(weight, codes, scales, hr, after)


def hessian_rows(row_chunks, cols, earlier, index, shape, scale, after):
    tokens, height = row_chunks[0].shape
    block = height * len(row_chunks)
    tile = min(512, cols.shape[1])
    count = len(row_chunks)
    ins = [*row_chunks, cols]
    specs = [pl.BlockSpec((tokens, height), lambda j: (0, 0))] * count
    specs.append(pl.BlockSpec((tokens, tile), lambda j: (0, j)))
    aliases = {}
    if earlier is not None:
        aliases = {len(ins): 0}
        ins.append(earlier)
        specs.append(pl.BlockSpec(memory_space=pl.ANY))
    for value in after:
        ins.append(value)
        specs.append(pl.BlockSpec(memory_space=pl.ANY))

    def kernel(*refs):
        cols_ref = refs[count]
        out_ref, turned_ref = refs[-2:]

        @pl.when(pl.program_id(0) == 0)
        def _():
            for chunk in range(count):
                turned_ref[chunk * height : (chunk + 1) * height] = refs[chunk][...].T

        total = jnp.dot(turned_ref[...], cols_ref[...], preferred_element_type=F32)
        out_ref[...] = (total * scale).astype(BF16)

    return pl.pallas_call(
        kernel,
        out_shape=jax.ShapeDtypeStruct(shape, BF16),
        grid=(cols.shape[1] // tile,),
        in_specs=specs,
        out_specs=pl.BlockSpec((block, tile), lambda j: (index, j)),
        scratch_shapes=[pltpu.VMEM((block, tokens), BF16)],
        input_output_aliases=aliases,
        compiler_params=pltpu.CompilerParams(vmem_limit_bytes=48 * MIB),
        name="hessian_rows",
    )(*ins)


def pair_sum(values):
    while len(values) > 1:
        values = [values[i] + values[i + 1] for i in range(0, len(values), 2)]
    return values[0]


def body(activations, weight_tile, codes, group_scales, right_factor):
    wide_count = lax.axis_size("wide")
    narrow_count = lax.axis_size("narrow")
    wide_index = lax.axis_index("wide")
    narrow_index = lax.axis_index("narrow")
    tokens, features = activations.shape
    rows = weight_tile.shape[0]
    split = features // rows
    scale = 1.0 / (tokens * wide_count)
    bits = [1 << b for b in range(1, wide_count.bit_length() - 1)]

    right_block = lax.dynamic_slice_in_dim(right_factor, narrow_index * features, features, 0)
    product = jnp.dot(activations, right_block, preferred_element_type=F32)
    product = pair_sum([product] + [flip(product, "narrow", m) for m in range(1, narrow_count)])
    y_blocks = product.astype(BF16)[None]
    mask = 1
    while mask < wide_count:
        y_blocks = jnp.concatenate([y_blocks, flip(y_blocks, "wide", mask)], axis=0)
        mask *= 2

    middle = features // 2
    pieces = []
    for half, order in enumerate((bits[::-1], bits)):
        held = {0: activations[:, half * middle : (half + 1) * middle]}
        for bit in order + [1]:
            held.update({m | bit: flip(held[m], "wide", bit) for m in list(held)})
        pieces += [held[m] for m in range(wide_count)]

    unit = rows // sum(PARTS)
    gathered = []
    at = 0
    for part in PARTS:
        height = part * unit
        mine = jnp.stack(
            [activations[:, s * rows + at : s * rows + at + height] for s in range(split)]
        )
        gathered.append(lax.all_gather(mine, "narrow", axis=0, tiled=True))
        at += height

    cols, hr, gram = columns_hr_gram(
        pieces, y_blocks, wide_index.astype(jnp.int32).reshape(1), scale
    )
    every = [hold(gathered[0], hr)]
    partial = residual_partial(weight_tile, codes, group_scales, hr, every[0])
    every += [hold(value, partial) for value in gathered[1:]]
    share = rows // narrow_count
    received = []
    for m in range(narrow_count):
        piece = lax.dynamic_slice_in_dim(partial, (narrow_index ^ m) * share, share, 0)
        received.append(flip(piece, "narrow", m) if m else piece)
    residual_product = pair_sum([piece.astype(F32) for piece in received])

    hessian = None
    at = 0
    for index, part in enumerate(PARTS):
        height = part * unit
        chunk = lax.all_to_all(every[index], "wide", split_axis=0, concat_axis=0, tiled=True)
        chunk = chunk.reshape(tokens * wide_count, height)
        hessian = hessian_rows(
            [chunk], cols, hessian, at // height, (rows, features), scale, [] if index else [partial]
        )
        at += height
    return residual_product, gram, hessian


def solution(mesh):
    in_specs = (
        P("wide", "narrow"),
        P("wide", "narrow"),
        P("wide", "narrow"),
        P("wide", "narrow"),
        P(),
    )
    out_specs = (P(("wide", "narrow"), None), P(), P("wide", "narrow"))
    return jax.shard_map(body, mesh=mesh, in_specs=in_specs, out_specs=out_specs, check_vma=False)
```

```python
import functools

import jax
import jax.numpy as jnp
from jax import lax
from jax.experimental import pallas as pl
from jax.experimental.pallas import tpu as pltpu
from jax.sharding import PartitionSpec as P

CHUNKS = 2
MIB = 1024 * 1024
BF16 = jnp.bfloat16
F32 = jnp.float32


def flip(value, axis, mask):
    count = lax.axis_size(axis)
    return lax.ppermute(value, axis, [(i, i ^ mask) for i in range(count)])


def cost(flops, moved):
    return pl.CostEstimate(flops=int(flops), bytes_accessed=int(moved), transcendentals=0)


def hr_and_gram(cols, y_blocks, where, scale):
    count, tokens, rank = y_blocks.shape
    features = cols.shape[1]
    tile = min(1024, features)

    def kernel(where_ref, cols_ref, y_ref, hr_ref, gram_ref, order_ref, turned_ref):
        @pl.when(pl.program_id(0) == 0)
        def _():
            for mask in range(count):
                at = pl.multiple_of((where_ref[0] ^ mask) * tokens, tokens)
                order_ref[pl.ds(at, tokens), :] = y_ref[mask]
            turned_ref[...] = order_ref[...].T
            gram = jnp.dot(turned_ref[...], order_ref[...], preferred_element_type=F32)
            gram_ref[...] = gram * scale

        total = jnp.dot(turned_ref[...], cols_ref[...], preferred_element_type=F32) * scale
        hr_ref[...] = total.T.astype(BF16)

    return pl.pallas_call(
        kernel,
        out_shape=(
            jax.ShapeDtypeStruct((features, rank), BF16),
            jax.ShapeDtypeStruct((rank, rank), F32),
        ),
        grid=(features // tile,),
        in_specs=[
            pl.BlockSpec(memory_space=pltpu.SMEM),
            pl.BlockSpec((count * tokens, tile), lambda j: (0, j)),
            pl.BlockSpec(y_blocks.shape, lambda j: (0, 0, 0)),
        ],
        out_specs=(
            pl.BlockSpec((tile, rank), lambda j: (j, 0)),
            pl.BlockSpec((rank, rank), lambda j: (0, 0)),
        ),
        scratch_shapes=[
            pltpu.VMEM((count * tokens, rank), BF16),
            pltpu.VMEM((rank, count * tokens), BF16),
        ],
        cost_estimate=cost(4 * count * tokens * features * rank, 4 * cols.size),
        compiler_params=pltpu.CompilerParams(vmem_limit_bytes=48 * MIB),
        name="hr_and_gram",
    )(where, cols, y_blocks)


def place_kernel(sources, where_ref, *refs):
    out_ref = refs[-1]
    count = len(sources)
    me = where_ref[0]
    for mask in range(count):
        other = me ^ mask
        near, far = sources[mask]

        def put(index, other=other):
            out_ref[other] = refs[index][...]

        if far is None:
            put(near)
        elif near is None:
            put(far)
        else:
            close = jnp.abs(me - other) <= count // 2
            pl.when(close)(functools.partial(put, near))
            pl.when(jnp.logical_not(close))(functools.partial(put, far))


def place_blocks(blocks, sources, where, after):
    count = len(sources)
    return pl.pallas_call(
        functools.partial(place_kernel, sources),
        out_shape=jax.ShapeDtypeStruct((count,) + blocks[0].shape, BF16),
        in_specs=[pl.BlockSpec(memory_space=pltpu.SMEM)]
        + [pl.BlockSpec(memory_space=pltpu.VMEM)] * len(blocks)
        + [pl.BlockSpec(memory_space=pl.ANY)] * len(after),
        out_specs=pl.BlockSpec(memory_space=pltpu.VMEM),
        cost_estimate=cost(0, 4 * count * blocks[0].size),
        compiler_params=pltpu.CompilerParams(vmem_limit_bytes=48 * MIB),
        name="place_blocks",
    )(where, *blocks, *after)


def exchange_blocks(mine):
    count = lax.axis_size("narrow")
    half = count // 2
    blocks = [mine]
    sources = [(0, None)]
    direct = {}
    order = sorted(range(1, count), key=lambda m: (m != half, m))
    for mask in order:
        pairs = [(i, i ^ mask) for i in range(count) if abs(i - (i ^ mask)) <= half]
        direct[mask] = lax.ppermute(mine, "narrow", pairs) if pairs else None
    for mask in range(1, count):
        near = far = None
        if direct[mask] is not None:
            near = len(blocks)
            blocks.append(direct[mask])
        pairs = [(i ^ half, i ^ mask) for i in range(count) if abs(i - (i ^ mask)) > half]
        if pairs:
            far = len(blocks)
            blocks.append(lax.ppermute(direct[half], "narrow", pairs))
        sources.append((near, far))
    return blocks, sources


def residual_kernel(weight_ref, codes_ref, scales_ref, hr_ref, after_ref, out_ref):
    groups = scales_ref.shape[1]
    width = weight_ref.shape[1] // groups
    scales = scales_ref[...]
    parts = []
    for group in range(groups):
        at = slice(group * width, (group + 1) * width)
        quantized = codes_ref[:, at].astype(F32) * scales[:, group : group + 1]
        parts.append((weight_ref[:, at].astype(F32) - quantized).astype(BF16))
    residual = jnp.concatenate(parts, axis=1)
    out_ref[...] = jnp.dot(residual, hr_ref[...], preferred_element_type=F32).astype(BF16)


def residual_partial(weight, codes, scales, hr, after):
    rows, features = weight.shape
    rank = hr.shape[1]
    block = min(256, rows)
    return pl.pallas_call(
        residual_kernel,
        out_shape=jax.ShapeDtypeStruct((rows, rank), BF16),
        grid=(rows // block,),
        in_specs=[
            pl.BlockSpec((block, features), lambda i: (i, 0)),
            pl.BlockSpec((block, features), lambda i: (i, 0)),
            pl.BlockSpec((block, scales.shape[1]), lambda i: (i, 0)),
            pl.BlockSpec((features, rank), lambda i: (0, 0)),
            pl.BlockSpec(memory_space=pl.ANY),
        ],
        out_specs=pl.BlockSpec((block, rank), lambda i: (i, 0)),
        cost_estimate=cost(4 * rows * features * rank, 8 * rows * features),
        compiler_params=pltpu.CompilerParams(vmem_limit_bytes=48 * MIB),
        name="residual_product",
    )(weight, codes, scales, hr, after)


def hessian_rows(row_chunks, cols, earlier, index, shape, scale, after):
    tokens, height = row_chunks[0].shape
    block = height * len(row_chunks)
    tile = min(512, cols.shape[1])
    count = len(row_chunks)
    ins = [*row_chunks, cols]
    specs = [pl.BlockSpec((tokens, height), lambda j: (0, 0))] * count
    specs.append(pl.BlockSpec((tokens, tile), lambda j: (0, j)))
    aliases = {}
    if earlier is not None:
        aliases = {len(ins): 0}
        ins.append(earlier)
        specs.append(pl.BlockSpec(memory_space=pl.ANY))
    for value in after:
        ins.append(value)
        specs.append(pl.BlockSpec(memory_space=pl.ANY))

    def kernel(*refs):
        cols_ref = refs[count]
        out_ref, turned_ref = refs[-2:]

        @pl.when(pl.program_id(0) == 0)
        def _():
            for chunk in range(count):
                turned_ref[chunk * height : (chunk + 1) * height] = refs[chunk][...].T

        total = jnp.dot(turned_ref[...], cols_ref[...], preferred_element_type=F32)
        out_ref[...] = (total * scale).astype(BF16)

    return pl.pallas_call(
        kernel,
        out_shape=jax.ShapeDtypeStruct(shape, BF16),
        grid=(cols.shape[1] // tile,),
        in_specs=specs,
        out_specs=pl.BlockSpec((block, tile), lambda j: (index, j)),
        scratch_shapes=[pltpu.VMEM((block, tokens), BF16)],
        input_output_aliases=aliases,
        cost_estimate=cost(
            4 * block * cols.size, 2 * cols.size + 2 * block * (tokens + cols.shape[1])
        ),
        compiler_params=pltpu.CompilerParams(vmem_limit_bytes=48 * MIB),
        name="hessian_rows",
    )(*ins)


def add_pieces(pieces, after):
    rows, rank = pieces[0].shape

    def kernel(*refs):
        total = refs[0][...].astype(F32)
        for ref in refs[1 : len(pieces)]:
            total += ref[...].astype(F32)
        refs[-1][...] = total

    return pl.pallas_call(
        kernel,
        out_shape=jax.ShapeDtypeStruct((rows, rank), F32),
        in_specs=[pl.BlockSpec(memory_space=pltpu.VMEM)] * len(pieces)
        + [pl.BlockSpec(memory_space=pl.ANY)],
        out_specs=pl.BlockSpec(memory_space=pltpu.VMEM),
        cost_estimate=cost(0, 12 * rows * rank),
        name="add_pieces",
    )(*pieces, after)


def pair_sum(values):
    while len(values) > 1:
        values = [values[i] + values[i + 1] for i in range(0, len(values), 2)]
    return values[0]


def body(activations, weight_tile, codes, group_scales, right_factor):
    wide_count = lax.axis_size("wide")
    narrow_count = lax.axis_size("narrow")
    wide_index = lax.axis_index("wide").astype(jnp.int32)
    narrow_index = lax.axis_index("narrow").astype(jnp.int32)
    tokens, features = activations.shape
    rows = weight_tile.shape[0]
    split = features // rows
    scale = 1.0 / (tokens * wide_count)

    cols = lax.all_gather(activations, "wide", axis=0, tiled=True)

    height = rows // CHUNKS
    chunks = []
    for chunk in range(CHUNKS):
        mine = jnp.stack(
            [
                activations[:, s * rows + chunk * height : s * rows + (chunk + 1) * height]
                for s in range(split)
            ]
        )
        chunks.append(exchange_blocks(mine))

    right_block = lax.dynamic_slice_in_dim(right_factor, narrow_index * features, features, 0)
    product = jnp.dot(activations, right_block, preferred_element_type=F32)
    product = pair_sum([product] + [flip(product, "narrow", m) for m in range(1, narrow_count)])
    y_blocks = product.astype(BF16)[None]
    mask = 1
    while mask < wide_count:
        y_blocks = jnp.concatenate([y_blocks, flip(y_blocks, "wide", mask)], axis=0)
        mask *= 2

    where = narrow_index.reshape(1)
    row_chunks = []
    placed = []
    for chunk in range(CHUNKS):
        blocks, sources = chunks[chunk]
        after = placed[-1:]
        every = place_blocks(blocks, sources, where, after)
        placed.append(every)
        every = every.reshape(narrow_count * split, tokens, height)
        chunk_rows = lax.all_to_all(every, "wide", split_axis=0, concat_axis=0, tiled=True)
        row_chunks.append(chunk_rows.reshape(tokens * wide_count, height))

    hr, gram = hr_and_gram(cols, y_blocks, wide_index.reshape(1), scale)
    partial = residual_partial(weight_tile, codes, group_scales, hr, placed[-1])
    share = rows // narrow_count
    received = []
    for m in range(narrow_count):
        piece = lax.dynamic_slice_in_dim(partial, (narrow_index ^ m) * share, share, 0)
        received.append(flip(piece, "narrow", m) if m else piece)

    hessian = None
    for chunk in range(CHUNKS):
        hessian = hessian_rows(
            [row_chunks[chunk]], cols, hessian, chunk, (rows, features), scale, [partial]
        )
    return add_pieces(received, hessian), gram, hessian


def solution(mesh):
    in_specs = (
        P("wide", "narrow"),
        P("wide", "narrow"),
        P("wide", "narrow"),
        P("wide", "narrow"),
        P(),
    )
    out_specs = (P(("wide", "narrow"), None), P(), P("wide", "narrow"))
    return jax.shard_map(body, mesh=mesh, in_specs=in_specs, out_specs=out_specs, check_vma=False)
```

```python
import functools

import jax
import jax.numpy as jnp
from jax import lax
from jax.experimental import pallas as pl
from jax.experimental.pallas import tpu as pltpu
from jax.sharding import PartitionSpec as P

CHUNKS = 2
MIB = 1024 * 1024
BF16 = jnp.bfloat16
F32 = jnp.float32


def flip(value, axis, mask):
    count = lax.axis_size(axis)
    return lax.ppermute(value, axis, [(i, i ^ mask) for i in range(count)])


def first_tile(value):
    shape = (1,) * (value.ndim - 2) + (16, 128)
    return pl.BlockSpec(shape, lambda *at: (0,) * value.ndim)


def cost(flops, moved):
    return pl.CostEstimate(flops=int(flops), bytes_accessed=int(moved), transcendentals=0)


def hr_and_gram(cols, y_blocks, where, scale):
    count, tokens, rank = y_blocks.shape
    features = cols.shape[1]
    tile = min(1024, features)

    def kernel(where_ref, cols_ref, y_ref, hr_ref, gram_ref, order_ref, turned_ref):
        @pl.when(pl.program_id(0) == 0)
        def _():
            for mask in range(count):
                at = pl.multiple_of((where_ref[0] ^ mask) * tokens, tokens)
                order_ref[pl.ds(at, tokens), :] = y_ref[mask]
            turned_ref[...] = order_ref[...].T
            gram = jnp.dot(turned_ref[...], order_ref[...], preferred_element_type=F32)
            gram_ref[...] = gram * scale

        total = jnp.dot(turned_ref[...], cols_ref[...], preferred_element_type=F32) * scale
        hr_ref[...] = total.T.astype(BF16)

    return pl.pallas_call(
        kernel,
        out_shape=(
            jax.ShapeDtypeStruct((features, rank), BF16),
            jax.ShapeDtypeStruct((rank, rank), F32),
        ),
        grid=(features // tile,),
        in_specs=[
            pl.BlockSpec(memory_space=pltpu.SMEM),
            pl.BlockSpec((count * tokens, tile), lambda j: (0, j)),
            pl.BlockSpec(y_blocks.shape, lambda j: (0, 0, 0)),
        ],
        out_specs=(
            pl.BlockSpec((tile, rank), lambda j: (j, 0)),
            pl.BlockSpec((rank, rank), lambda j: (0, 0)),
        ),
        scratch_shapes=[
            pltpu.VMEM((count * tokens, rank), BF16),
            pltpu.VMEM((rank, count * tokens), BF16),
        ],
        cost_estimate=cost(4 * count * tokens * features * rank, 4 * cols.size),
        compiler_params=pltpu.CompilerParams(vmem_limit_bytes=48 * MIB),
        name="hr_and_gram",
    )(where, cols, y_blocks)


def place_kernel(sources, where_ref, *refs):
    out_ref = refs[-1]
    count = len(sources)
    me = where_ref[0]
    for mask in range(count):
        other = me ^ mask
        near, far = sources[mask]

        def put(index, other=other):
            out_ref[other] = refs[index][...]

        if far is None:
            put(near)
        elif near is None:
            put(far)
        else:
            close = jnp.abs(me - other) <= count // 2
            pl.when(close)(functools.partial(put, near))
            pl.when(jnp.logical_not(close))(functools.partial(put, far))


def place_blocks(blocks, sources, where, after):
    count = len(sources)
    return pl.pallas_call(
        functools.partial(place_kernel, sources),
        out_shape=jax.ShapeDtypeStruct((count,) + blocks[0].shape, BF16),
        grid=(1,),
        in_specs=[pl.BlockSpec(memory_space=pltpu.SMEM)]
        + [pl.BlockSpec(memory_space=pltpu.VMEM)] * len(blocks)
        + [first_tile(value) for value in after],
        out_specs=pl.BlockSpec(memory_space=pltpu.VMEM),
        cost_estimate=cost(0, 4 * count * blocks[0].size),
        compiler_params=pltpu.CompilerParams(vmem_limit_bytes=48 * MIB),
        name="place_blocks",
    )(where, *blocks, *after)


def take_chunk(activations, chunk, height, split, after):
    tokens, features = activations.shape
    rows = features // split

    def kernel(activations_ref, *refs):
        for s in range(split):
            at = s * rows + chunk * height
            refs[-1][s] = activations_ref[:, at : at + height]

    return pl.pallas_call(
        kernel,
        out_shape=jax.ShapeDtypeStruct((split, tokens, height), BF16),
        grid=(1,),
        in_specs=[pl.BlockSpec((tokens, features), lambda i: (0, 0))]
        + [first_tile(value) for value in after],
        out_specs=pl.BlockSpec((split, tokens, height), lambda i: (0, 0, 0)),
        cost_estimate=cost(0, 4 * split * tokens * height),
        name="take_chunk",
    )(activations, *after)


def exchange_blocks(mine):
    count = lax.axis_size("narrow")
    half = count // 2
    blocks = [mine]
    sources = [(0, None)]
    direct = {}
    order = sorted(range(1, count), key=lambda m: (m != half, m))
    for mask in order:
        pairs = [(i, i ^ mask) for i in range(count) if abs(i - (i ^ mask)) <= half]
        direct[mask] = lax.ppermute(mine, "narrow", pairs) if pairs else None
    for mask in range(1, count):
        near = far = None
        if direct[mask] is not None:
            near = len(blocks)
            blocks.append(direct[mask])
        pairs = [(i ^ half, i ^ mask) for i in range(count) if abs(i - (i ^ mask)) > half]
        if pairs:
            far = len(blocks)
            blocks.append(lax.ppermute(direct[half], "narrow", pairs))
        sources.append((near, far))
    return blocks, sources


def residual_kernel(weight_ref, codes_ref, scales_ref, hr_ref, *refs):
    out_ref = refs[-1]
    groups = scales_ref.shape[1]
    width = weight_ref.shape[1] // groups
    scales = scales_ref[...]
    parts = []
    for group in range(groups):
        at = slice(group * width, (group + 1) * width)
        quantized = codes_ref[:, at].astype(F32) * scales[:, group : group + 1]
        parts.append((weight_ref[:, at].astype(F32) - quantized).astype(BF16))
    residual = jnp.concatenate(parts, axis=1)
    out_ref[...] = jnp.dot(residual, hr_ref[...], preferred_element_type=F32).astype(BF16)


def residual_partial(weight, codes, scales, hr, part, count, after):
    rows, features = weight.shape
    rank = hr.shape[1]
    rows //= count
    block = min(256, rows)
    first = part * (rows // block)
    return pl.pallas_call(
        residual_kernel,
        out_shape=jax.ShapeDtypeStruct((rows, rank), BF16),
        grid=(rows // block,),
        in_specs=[
            pl.BlockSpec((block, features), lambda i: (first + i, 0)),
            pl.BlockSpec((block, features), lambda i: (first + i, 0)),
            pl.BlockSpec((block, scales.shape[1]), lambda i: (first + i, 0)),
            pl.BlockSpec((features, rank), lambda i: (0, 0)),
        ]
        + [first_tile(value) for value in after],
        out_specs=pl.BlockSpec((block, rank), lambda i: (i, 0)),
        cost_estimate=cost(4 * rows * features * rank, 8 * rows * features),
        compiler_params=pltpu.CompilerParams(vmem_limit_bytes=48 * MIB),
        name="residual_product",
    )(weight, codes, scales, hr, *after)


def hessian_rows(row_chunks, cols, earlier, index, shape, scale, after):
    tokens, height = row_chunks[0].shape
    block = height * len(row_chunks)
    tile = min(512, cols.shape[1])
    count = len(row_chunks)
    ins = [*row_chunks, cols]
    specs = [pl.BlockSpec((tokens, height), lambda j: (0, 0))] * count
    specs.append(pl.BlockSpec((tokens, tile), lambda j: (0, j)))
    aliases = {}
    if earlier is not None:
        aliases = {len(ins): 0}
        ins.append(earlier)
        specs.append(pl.BlockSpec(memory_space=pl.ANY))
    for value in after:
        ins.append(value)
        specs.append(first_tile(value))

    def kernel(*refs):
        cols_ref = refs[count]
        out_ref, turned_ref = refs[-2:]

        @pl.when(pl.program_id(0) == 0)
        def _():
            for chunk in range(count):
                turned_ref[chunk * height : (chunk + 1) * height] = refs[chunk][...].T

        total = jnp.dot(turned_ref[...], cols_ref[...], preferred_element_type=F32)
        out_ref[...] = (total * scale).astype(BF16)

    return pl.pallas_call(
        kernel,
        out_shape=jax.ShapeDtypeStruct(shape, BF16),
        grid=(cols.shape[1] // tile,),
        in_specs=specs,
        out_specs=pl.BlockSpec((block, tile), lambda j: (index, j)),
        scratch_shapes=[pltpu.VMEM((block, tokens), BF16)],
        input_output_aliases=aliases,
        cost_estimate=cost(
            4 * block * cols.size, 2 * cols.size + 2 * block * (tokens + cols.shape[1])
        ),
        compiler_params=pltpu.CompilerParams(vmem_limit_bytes=48 * MIB),
        name="hessian_rows",
    )(*ins)


def add_pieces(pieces, after):
    rows, rank = pieces[0].shape

    def kernel(*refs):
        total = refs[0][...].astype(F32)
        for ref in refs[1 : len(pieces)]:
            total += ref[...].astype(F32)
        refs[-1][...] = total

    return pl.pallas_call(
        kernel,
        out_shape=jax.ShapeDtypeStruct((rows, rank), F32),
        grid=(1,),
        in_specs=[pl.BlockSpec(memory_space=pltpu.VMEM)] * len(pieces)
        + [first_tile(after)],
        out_specs=pl.BlockSpec(memory_space=pltpu.VMEM),
        cost_estimate=cost(0, 12 * rows * rank),
        name="add_pieces",
    )(*pieces, after)


def pair_sum(values):
    while len(values) > 1:
        values = [values[i] + values[i + 1] for i in range(0, len(values), 2)]
    return values[0]


def body(activations, weight_tile, codes, group_scales, right_factor):
    wide_count = lax.axis_size("wide")
    narrow_count = lax.axis_size("narrow")
    wide_index = lax.axis_index("wide").astype(jnp.int32)
    narrow_index = lax.axis_index("narrow").astype(jnp.int32)
    tokens, features = activations.shape
    rows = weight_tile.shape[0]
    split = features // rows
    scale = 1.0 / (tokens * wide_count)

    cols = lax.all_gather(activations, "wide", axis=0, tiled=True)

    right_block = lax.dynamic_slice_in_dim(right_factor, narrow_index * features, features, 0)
    product = jnp.dot(activations, right_block, preferred_element_type=F32)
    product = pair_sum([product] + [flip(product, "narrow", m) for m in range(1, narrow_count)])
    steps = [product]
    y_blocks = product.astype(BF16)[None]
    mask = 1
    while mask < wide_count:
        y_blocks = jnp.concatenate([y_blocks, flip(y_blocks, "wide", mask)], axis=0)
        steps.append(y_blocks)
        mask *= 2

    height = rows // CHUNKS
    chunks = []
    after = []
    for chunk in range(CHUNKS):
        chunks.append(exchange_blocks(take_chunk(activations, chunk, height, split, after)))
        after = [steps[0], chunks[-1][0][-1 if narrow_count < 4 else narrow_count // 2]]

    where = narrow_index.reshape(1)
    row_chunks = []
    placed = []
    for chunk in range(CHUNKS):
        blocks, sources = chunks[chunk]
        after = placed[-1:] if chunk else steps[-2:-1]
        every = place_blocks(blocks, sources, where, after)
        placed.append(every)
        every = every.reshape(narrow_count * split, tokens, height)
        chunk_rows = lax.all_to_all(every, "wide", split_axis=0, concat_axis=0, tiled=True)
        row_chunks.append(chunk_rows.reshape(tokens * wide_count, height))

    hr, gram = hr_and_gram(cols, y_blocks, wide_index.reshape(1), scale)
    partial = []
    for part in range(2):
        after = [placed[-1], partial[0]] if part else []
        partial.append(
            residual_partial(weight_tile, codes, group_scales, hr, part, 2, after)
        )
    partial = jnp.concatenate(partial, axis=0)
    share = rows // narrow_count
    received = []
    for m in range(narrow_count):
        piece = lax.dynamic_slice_in_dim(partial, (narrow_index ^ m) * share, share, 0)
        received.append(flip(piece, "narrow", m) if m else piece)

    hessian = None
    for chunk in range(CHUNKS):
        hessian = hessian_rows(
            [row_chunks[chunk]], cols, hessian, chunk, (rows, features), scale, [partial]
        )
    return add_pieces(received, hessian), gram, hessian


def solution(mesh):
    in_specs = (
        P("wide", "narrow"),
        P("wide", "narrow"),
        P("wide", "narrow"),
        P("wide", "narrow"),
        P(),
    )
    out_specs = (P(("wide", "narrow"), None), P(), P("wide", "narrow"))
    return jax.shard_map(body, mesh=mesh, in_specs=in_specs, out_specs=out_specs, check_vma=False)
```

```python
import functools

import jax
import jax.numpy as jnp
from jax import lax
from jax.experimental import pallas as pl
from jax.experimental.pallas import tpu as pltpu
from jax.sharding import PartitionSpec as P

CHUNKS = 2
MIB = 1024 * 1024
BF16 = jnp.bfloat16
F32 = jnp.float32


def flip(value, axis, mask):
    count = lax.axis_size(axis)
    return lax.ppermute(value, axis, [(i, i ^ mask) for i in range(count)])


def first_tile(value):
    shape = (1,) * (value.ndim - 2) + (16, 128)
    return pl.BlockSpec(shape, lambda *at: (0,) * value.ndim)


def cost(flops, moved):
    return pl.CostEstimate(flops=int(flops), bytes_accessed=int(moved), transcendentals=0)


def hr_and_gram(cols, y_blocks, where, scale):
    count, tokens, rank = y_blocks.shape
    features = cols.shape[1]
    tile = min(1024, features)

    def kernel(where_ref, cols_ref, y_ref, hr_ref, gram_ref, order_ref, turned_ref):
        @pl.when(pl.program_id(0) == 0)
        def _():
            for mask in range(count):
                at = pl.multiple_of((where_ref[0] ^ mask) * tokens, tokens)
                order_ref[pl.ds(at, tokens), :] = y_ref[mask]
            turned_ref[...] = order_ref[...].T
            gram = jnp.dot(turned_ref[...], order_ref[...], preferred_element_type=F32)
            gram_ref[...] = gram * scale

        total = jnp.dot(turned_ref[...], cols_ref[...], preferred_element_type=F32) * scale
        hr_ref[...] = total.T.astype(BF16)

    return pl.pallas_call(
        kernel,
        out_shape=(
            jax.ShapeDtypeStruct((features, rank), BF16),
            jax.ShapeDtypeStruct((rank, rank), F32),
        ),
        grid=(features // tile,),
        in_specs=[
            pl.BlockSpec(memory_space=pltpu.SMEM),
            pl.BlockSpec((count * tokens, tile), lambda j: (0, j)),
            pl.BlockSpec(y_blocks.shape, lambda j: (0, 0, 0)),
        ],
        out_specs=(
            pl.BlockSpec((tile, rank), lambda j: (j, 0)),
            pl.BlockSpec((rank, rank), lambda j: (0, 0)),
        ),
        scratch_shapes=[
            pltpu.VMEM((count * tokens, rank), BF16),
            pltpu.VMEM((rank, count * tokens), BF16),
        ],
        cost_estimate=cost(4 * count * tokens * features * rank, 4 * cols.size),
        compiler_params=pltpu.CompilerParams(vmem_limit_bytes=48 * MIB),
        name="hr_and_gram",
    )(where, cols, y_blocks)


def place_kernel(sources, where_ref, *refs):
    out_ref = refs[-1]
    count = len(sources)
    me = where_ref[0]
    for mask in range(count):
        other = me ^ mask
        near, far = sources[mask]

        def put(index, other=other):
            out_ref[other] = refs[index][...]

        if far is None:
            put(near)
        elif near is None:
            put(far)
        else:
            close = jnp.abs(me - other) <= count // 2
            pl.when(close)(functools.partial(put, near))
            pl.when(jnp.logical_not(close))(functools.partial(put, far))


def place_blocks(blocks, sources, where, after):
    count = len(sources)
    return pl.pallas_call(
        functools.partial(place_kernel, sources),
        out_shape=jax.ShapeDtypeStruct((count,) + blocks[0].shape, BF16),
        grid=(1,),
        in_specs=[pl.BlockSpec(memory_space=pltpu.SMEM)]
        + [pl.BlockSpec(memory_space=pltpu.VMEM)] * len(blocks)
        + [first_tile(value) for value in after],
        out_specs=pl.BlockSpec(memory_space=pltpu.VMEM),
        cost_estimate=cost(0, 4 * count * blocks[0].size),
        compiler_params=pltpu.CompilerParams(vmem_limit_bytes=48 * MIB),
        name="place_blocks",
    )(where, *blocks, *after)


def take_chunk(activations, chunk, height, split, after):
    tokens, features = activations.shape
    rows = features // split

    def kernel(activations_ref, *refs):
        for s in range(split):
            at = s * rows + chunk * height
            refs[-1][s] = activations_ref[:, at : at + height]

    return pl.pallas_call(
        kernel,
        out_shape=jax.ShapeDtypeStruct((split, tokens, height), BF16),
        grid=(1,),
        in_specs=[pl.BlockSpec((tokens, features), lambda i: (0, 0))]
        + [first_tile(value) for value in after],
        out_specs=pl.BlockSpec((split, tokens, height), lambda i: (0, 0, 0)),
        cost_estimate=cost(0, 4 * split * tokens * height),
        name="take_chunk",
    )(activations, *after)


def exchange_blocks(mine):
    count = lax.axis_size("narrow")
    half = count // 2
    blocks = [mine]
    sources = [(0, None)]
    direct = {}
    order = sorted(range(1, count), key=lambda m: (m != half, m))
    for mask in order:
        pairs = [(i, i ^ mask) for i in range(count) if abs(i - (i ^ mask)) <= half]
        direct[mask] = lax.ppermute(mine, "narrow", pairs) if pairs else None
    for mask in range(1, count):
        near = far = None
        if direct[mask] is not None:
            near = len(blocks)
            blocks.append(direct[mask])
        pairs = [(i ^ half, i ^ mask) for i in range(count) if abs(i - (i ^ mask)) > half]
        if pairs:
            far = len(blocks)
            blocks.append(lax.ppermute(direct[half], "narrow", pairs))
        sources.append((near, far))
    return blocks, sources


def residual_kernel(weight_ref, codes_ref, scales_ref, hr_ref, *refs):
    out_ref = refs[-1]
    groups = scales_ref.shape[1]
    width = weight_ref.shape[1] // groups
    scales = scales_ref[...]
    parts = []
    for group in range(groups):
        at = slice(group * width, (group + 1) * width)
        quantized = codes_ref[:, at].astype(F32) * scales[:, group : group + 1]
        parts.append((weight_ref[:, at].astype(F32) - quantized).astype(BF16))
    residual = jnp.concatenate(parts, axis=1)
    out_ref[...] = jnp.dot(residual, hr_ref[...], preferred_element_type=F32).astype(BF16)


def residual_partial(weight, codes, scales, hr, earlier, part, count, after):
    features = weight.shape[1]
    rank = hr.shape[1]
    rows = weight.shape[0] // count
    block = min(256, rows)
    first = part * (rows // block)
    ins = [weight, codes, scales, hr]
    aliases = {}
    if earlier is not None:
        aliases = {len(ins): 0}
        ins.append(earlier)
    return pl.pallas_call(
        residual_kernel,
        out_shape=jax.ShapeDtypeStruct((weight.shape[0], rank), BF16),
        grid=(rows // block,),
        in_specs=[
            pl.BlockSpec((block, features), lambda i: (first + i, 0)),
            pl.BlockSpec((block, features), lambda i: (first + i, 0)),
            pl.BlockSpec((block, scales.shape[1]), lambda i: (first + i, 0)),
            pl.BlockSpec((features, rank), lambda i: (0, 0)),
        ]
        + [pl.BlockSpec(memory_space=pl.ANY)] * len(aliases)
        + [first_tile(value) for value in after],
        out_specs=pl.BlockSpec((block, rank), lambda i: (first + i, 0)),
        input_output_aliases=aliases,
        cost_estimate=cost(4 * rows * features * rank, 8 * rows * features),
        compiler_params=pltpu.CompilerParams(vmem_limit_bytes=48 * MIB),
        name="residual_product",
    )(*ins, *after)


def hessian_rows(row_chunks, cols, earlier, index, shape, scale, after):
    tokens, height = row_chunks[0].shape
    block = height * len(row_chunks)
    tile = min(1024, cols.shape[1])
    count = len(row_chunks)
    ins = [*row_chunks, cols]
    specs = [pl.BlockSpec((tokens, height), lambda j: (0, 0))] * count
    specs.append(pl.BlockSpec((tokens, tile), lambda j: (0, j)))
    aliases = {}
    if earlier is not None:
        aliases = {len(ins): 0}
        ins.append(earlier)
        specs.append(pl.BlockSpec(memory_space=pl.ANY))
    for value in after:
        ins.append(value)
        specs.append(first_tile(value))

    def kernel(*refs):
        cols_ref = refs[count]
        out_ref, turned_ref = refs[-2:]

        @pl.when(pl.program_id(0) == 0)
        def _():
            for chunk in range(count):
                turned_ref[chunk * height : (chunk + 1) * height] = refs[chunk][...].T

        total = jnp.dot(turned_ref[...], cols_ref[...], preferred_element_type=F32)
        out_ref[...] = (total * scale).astype(BF16)

    return pl.pallas_call(
        kernel,
        out_shape=jax.ShapeDtypeStruct(shape, BF16),
        grid=(cols.shape[1] // tile,),
        in_specs=specs,
        out_specs=pl.BlockSpec((block, tile), lambda j: (index, j)),
        scratch_shapes=[pltpu.VMEM((block, tokens), BF16)],
        input_output_aliases=aliases,
        cost_estimate=cost(
            4 * block * cols.size, 2 * cols.size + 2 * block * (tokens + cols.shape[1])
        ),
        compiler_params=pltpu.CompilerParams(vmem_limit_bytes=48 * MIB),
        name="hessian_rows",
    )(*ins)


def add_pieces(pieces, after):
    rows, rank = pieces[0].shape

    def kernel(*refs):
        total = refs[0][...].astype(F32)
        for ref in refs[1 : len(pieces)]:
            total += ref[...].astype(F32)
        refs[-1][...] = total

    return pl.pallas_call(
        kernel,
        out_shape=jax.ShapeDtypeStruct((rows, rank), F32),
        grid=(1,),
        in_specs=[pl.BlockSpec(memory_space=pltpu.VMEM)] * len(pieces)
        + [first_tile(after)],
        out_specs=pl.BlockSpec(memory_space=pltpu.VMEM),
        cost_estimate=cost(0, 12 * rows * rank),
        name="add_pieces",
    )(*pieces, after)


def pair_sum(values):
    while len(values) > 1:
        values = [values[i] + values[i + 1] for i in range(0, len(values), 2)]
    return values[0]


def body(activations, weight_tile, codes, group_scales, right_factor):
    wide_count = lax.axis_size("wide")
    narrow_count = lax.axis_size("narrow")
    wide_index = lax.axis_index("wide").astype(jnp.int32)
    narrow_index = lax.axis_index("narrow").astype(jnp.int32)
    tokens, features = activations.shape
    rows = weight_tile.shape[0]
    split = features // rows
    scale = 1.0 / (tokens * wide_count)

    cols = lax.all_gather(activations, "wide", axis=0, tiled=True)

    right_block = lax.dynamic_slice_in_dim(right_factor, narrow_index * features, features, 0)
    own = jnp.dot(activations, right_block, preferred_element_type=F32)
    product = pair_sum([own] + [flip(own, "narrow", m) for m in range(1, narrow_count)])
    y_blocks = product.astype(BF16)[None]
    mask = 1
    while mask < wide_count:
        y_blocks = jnp.concatenate([y_blocks, flip(y_blocks, "wide", mask)], axis=0)
        mask *= 2

    height = rows // CHUNKS
    chunks = []
    after = [own]
    for chunk in range(CHUNKS):
        chunks.append(exchange_blocks(take_chunk(activations, chunk, height, split, after)))
        after = [chunks[-1][0][near] for near, _ in chunks[-1][1] if near]

    where = narrow_index.reshape(1)
    row_chunks = []
    placed = []
    for chunk in range(CHUNKS):
        blocks, sources = chunks[chunk]
        after = placed[-1:] if chunk else [y_blocks]
        every = place_blocks(blocks, sources, where, after)
        placed.append(every)
        every = every.reshape(narrow_count * split, tokens, height)
        chunk_rows = lax.all_to_all(every, "wide", split_axis=0, concat_axis=0, tiled=True)
        row_chunks.append(chunk_rows.reshape(tokens * wide_count, height))

    hr, gram = hr_and_gram(cols, y_blocks, wide_index.reshape(1), scale)
    partial = None
    for part in range(2):
        after = placed[-1:] if part else []
        partial = residual_partial(
            weight_tile, codes, group_scales, hr, partial, part, 2, after
        )
    share = rows // narrow_count
    received = []
    for m in range(narrow_count):
        piece = lax.dynamic_slice_in_dim(partial, (narrow_index ^ m) * share, share, 0)
        received.append(flip(piece, "narrow", m) if m else piece)

    hessian = None
    for chunk in range(CHUNKS):
        hessian = hessian_rows(
            [row_chunks[chunk]], cols, hessian, chunk, (rows, features), scale, [partial]
        )
    return add_pieces(received, hessian), gram, hessian


def solution(mesh):
    in_specs = (
        P("wide", "narrow"),
        P("wide", "narrow"),
        P("wide", "narrow"),
        P("wide", "narrow"),
        P(),
    )
    out_specs = (P(("wide", "narrow"), None), P(), P("wide", "narrow"))
    return jax.shard_map(body, mesh=mesh, in_specs=in_specs, out_specs=out_specs, check_vma=False)
```

```python
import functools

import jax
import jax.numpy as jnp
from jax import lax
from jax.experimental import pallas as pl
from jax.experimental.pallas import tpu as pltpu
from jax.sharding import PartitionSpec as P

CHUNKS = 2
MIB = 1024 * 1024
BF16 = jnp.bfloat16
F32 = jnp.float32


def flip(value, axis, mask):
    count = lax.axis_size(axis)
    return lax.ppermute(value, axis, [(i, i ^ mask) for i in range(count)])


def first_tile(value):
    shape = (1,) * (value.ndim - 2) + (16, 128)
    return pl.BlockSpec(shape, lambda *at: (0,) * value.ndim)


def cost(flops, moved):
    return pl.CostEstimate(flops=int(flops), bytes_accessed=int(moved), transcendentals=0)


def hr_and_gram(cols, y_blocks, where, scale):
    count, tokens, rank = y_blocks.shape
    features = cols.shape[1]
    tile = min(1024, features)

    def kernel(where_ref, cols_ref, y_ref, hr_ref, gram_ref, order_ref, turned_ref):
        @pl.when(pl.program_id(0) == 0)
        def _():
            for mask in range(count):
                at = pl.multiple_of((where_ref[0] ^ mask) * tokens, tokens)
                order_ref[pl.ds(at, tokens), :] = y_ref[mask]
            turned_ref[...] = order_ref[...].T
            gram = jnp.dot(turned_ref[...], order_ref[...], preferred_element_type=F32)
            gram_ref[...] = gram * scale

        total = jnp.dot(turned_ref[...], cols_ref[...], preferred_element_type=F32) * scale
        hr_ref[...] = total.T.astype(BF16)

    return pl.pallas_call(
        kernel,
        out_shape=(
            jax.ShapeDtypeStruct((features, rank), BF16),
            jax.ShapeDtypeStruct((rank, rank), F32),
        ),
        grid=(features // tile,),
        in_specs=[
            pl.BlockSpec(memory_space=pltpu.SMEM),
            pl.BlockSpec((count * tokens, tile), lambda j: (0, j)),
            pl.BlockSpec(y_blocks.shape, lambda j: (0, 0, 0)),
        ],
        out_specs=(
            pl.BlockSpec((tile, rank), lambda j: (j, 0)),
            pl.BlockSpec((rank, rank), lambda j: (0, 0)),
        ),
        scratch_shapes=[
            pltpu.VMEM((count * tokens, rank), BF16),
            pltpu.VMEM((rank, count * tokens), BF16),
        ],
        cost_estimate=cost(4 * count * tokens * features * rank, 4 * cols.size),
        compiler_params=pltpu.CompilerParams(vmem_limit_bytes=48 * MIB),
        name="hr_and_gram",
    )(where, cols, y_blocks)


def place_kernel(sources, where_ref, *refs):
    out_ref = refs[-1]
    count = len(sources)
    me = where_ref[0]
    for mask in range(count):
        other = me ^ mask
        near, far = sources[mask]

        def put(index, other=other):
            out_ref[other] = refs[index][:, :, : out_ref.shape[3]]

        if far is None:
            put(near)
        elif near is None:
            put(far)
        else:
            close = jnp.abs(me - other) <= count // 2
            pl.when(close)(functools.partial(put, near))
            pl.when(jnp.logical_not(close))(functools.partial(put, far))


def place_blocks(blocks, sources, where, height, after):
    count = len(sources)
    return pl.pallas_call(
        functools.partial(place_kernel, sources),
        out_shape=jax.ShapeDtypeStruct((count,) + blocks[0].shape[:2] + (height,), BF16),
        grid=(1,),
        in_specs=[pl.BlockSpec(memory_space=pltpu.SMEM)]
        + [pl.BlockSpec(memory_space=pltpu.VMEM)] * len(blocks)
        + [first_tile(value) for value in after],
        out_specs=pl.BlockSpec(memory_space=pltpu.VMEM),
        cost_estimate=cost(0, 4 * count * blocks[0].size),
        compiler_params=pltpu.CompilerParams(vmem_limit_bytes=48 * MIB),
        name="place_blocks",
    )(where, *blocks, *after)


def take_chunk(activations, chunk, height, split, tail, after):
    tokens, features = activations.shape
    rows = features // split
    share = tail[0].shape[1] // split if tail else 0

    def kernel(activations_ref, *refs):
        for s in range(split):
            at = s * rows + chunk * height
            refs[-1][s, :, :height] = activations_ref[:, at : at + height]
            if tail:
                refs[-1][s, :, height:] = refs[0][:, s * share : (s + 1) * share].astype(BF16)

    shape = (split, tokens, height + share)
    return pl.pallas_call(
        kernel,
        out_shape=jax.ShapeDtypeStruct(shape, BF16),
        grid=(1,),
        in_specs=[pl.BlockSpec((tokens, features), lambda i: (0, 0))]
        + [pl.BlockSpec(value.shape, lambda i: (0, 0)) for value in tail]
        + [first_tile(value) for value in after],
        out_specs=pl.BlockSpec(shape, lambda i: (0, 0, 0)),
        cost_estimate=cost(0, 4 * split * tokens * height),
        name="take_chunk",
    )(activations, *tail, *after)


def sum_tails(blocks, sources, where, height):
    split, tokens, width = blocks[0].shape
    share = width - height
    count = len(sources)
    spec = pl.BlockSpec((split, tokens, share), lambda i: (0, 0, height // share))

    def kernel(where_ref, *refs):
        out_ref, held_ref = refs[-2:]
        me = where_ref[0]
        for mask in range(count):
            near, far = sources[mask]

            def put(index, mask=mask):
                held_ref[mask] = refs[index][...].astype(F32)

            if far is None:
                put(near)
            elif near is None:
                put(far)
            else:
                close = jnp.abs(me - (me ^ mask)) <= count // 2
                pl.when(close)(functools.partial(put, near))
                pl.when(jnp.logical_not(close))(functools.partial(put, far))
        total = pair_sum([held_ref[mask] for mask in range(count)])
        for s in range(split):
            out_ref[0, :, s * share : (s + 1) * share] = total[s].astype(BF16)

    return pl.pallas_call(
        kernel,
        out_shape=jax.ShapeDtypeStruct((1, tokens, split * share), BF16),
        grid=(1,),
        in_specs=[pl.BlockSpec(memory_space=pltpu.SMEM)] + [spec] * len(blocks),
        out_specs=pl.BlockSpec((1, tokens, split * share), lambda i: (0, 0, 0)),
        scratch_shapes=[pltpu.VMEM((count, split, tokens, share), F32)],
        cost_estimate=cost(0, 4 * count * split * tokens * share),
        name="sum_tails",
    )(where, *blocks)


def relay(value, after):
    def kernel(value_ref, *refs):
        refs[-1][...] = value_ref[...]

    spec = pl.BlockSpec(value.shape, lambda i: (0, 0, 0))
    return pl.pallas_call(
        kernel,
        out_shape=jax.ShapeDtypeStruct(value.shape, value.dtype),
        grid=(1,),
        in_specs=[spec] + [first_tile(other) for other in after],
        out_specs=spec,
        cost_estimate=cost(0, 4 * value.size),
        name="relay",
    )(value, *after)


def exchange_blocks(mine, after):
    count = lax.axis_size("narrow")
    half = count // 2
    blocks = [mine]
    sources = [(0, None)]
    direct = {}
    order = sorted(range(1, count), key=lambda m: (m != half, m))
    for mask in order:
        pairs = [(i, i ^ mask) for i in range(count) if abs(i - (i ^ mask)) <= half]
        direct[mask] = lax.ppermute(mine, "narrow", pairs) if pairs else None
    onward = direct.get(half)
    if after and count > 2:
        onward = relay(onward, after)
    for mask in range(1, count):
        near = far = None
        if direct[mask] is not None:
            near = len(blocks)
            blocks.append(direct[mask])
        pairs = [(i ^ half, i ^ mask) for i in range(count) if abs(i - (i ^ mask)) > half]
        if pairs:
            far = len(blocks)
            blocks.append(lax.ppermute(onward, "narrow", pairs))
        sources.append((near, far))
    return blocks, sources


def residual_kernel(weight_ref, codes_ref, scales_ref, out_ref):
    groups = scales_ref.shape[1]
    width = weight_ref.shape[1] // groups
    scales = scales_ref[...]
    parts = []
    for group in range(groups):
        at = slice(group * width, (group + 1) * width)
        quantized = codes_ref[:, at].astype(F32) * scales[:, group : group + 1]
        parts.append((weight_ref[:, at].astype(F32) - quantized).astype(BF16))
    out_ref[...] = jnp.concatenate(parts, axis=1)


def residual_tile(weight, codes, scales):
    rows, features = weight.shape
    block = min(256, rows)
    return pl.pallas_call(
        residual_kernel,
        out_shape=jax.ShapeDtypeStruct((rows, features), BF16),
        grid=(rows // block,),
        in_specs=[
            pl.BlockSpec((block, features), lambda i: (i, 0)),
            pl.BlockSpec((block, features), lambda i: (i, 0)),
            pl.BlockSpec((block, scales.shape[1]), lambda i: (i, 0)),
        ],
        out_specs=pl.BlockSpec((block, features), lambda i: (i, 0)),
        compiler_params=pltpu.CompilerParams(vmem_limit_bytes=48 * MIB),
        cost_estimate=cost(0, 11 * rows * features),
        name="residual_tile",
    )(weight, codes, scales)


def product_kernel(residual_ref, hr_ref, out_ref):
    out_ref[...] = jnp.dot(residual_ref[...], hr_ref[...], preferred_element_type=F32).astype(BF16)


def partial_product(residual, hr):
    rows, features = residual.shape
    rank = hr.shape[1]
    block = min(512, rows)
    return pl.pallas_call(
        product_kernel,
        out_shape=jax.ShapeDtypeStruct((rows, rank), BF16),
        grid=(rows // block,),
        in_specs=[
            pl.BlockSpec((block, features), lambda i: (i, 0)),
            pl.BlockSpec((features, rank), lambda i: (0, 0)),
        ],
        out_specs=pl.BlockSpec((block, rank), lambda i: (i, 0)),
        compiler_params=pltpu.CompilerParams(vmem_limit_bytes=48 * MIB),
        cost_estimate=cost(4 * rows * features * rank, 3 * rows * features),
        name="partial_product",
    )(residual, hr)


def hessian_rows(row_chunks, cols, earlier, index, shape, scale, after):
    tokens, height = row_chunks[0].shape
    block = height * len(row_chunks)
    tile = min(1024, cols.shape[1])
    count = len(row_chunks)
    ins = [*row_chunks, cols]
    specs = [pl.BlockSpec((tokens, height), lambda j: (0, 0))] * count
    specs.append(pl.BlockSpec((tokens, tile), lambda j: (0, j)))
    aliases = {}
    if earlier is not None:
        aliases = {len(ins): 0}
        ins.append(earlier)
        specs.append(pl.BlockSpec(memory_space=pl.ANY))
    for value in after:
        ins.append(value)
        specs.append(first_tile(value))

    def kernel(*refs):
        cols_ref = refs[count]
        out_ref, turned_ref = refs[-2:]

        @pl.when(pl.program_id(0) == 0)
        def _():
            for chunk in range(count):
                turned_ref[chunk * height : (chunk + 1) * height] = refs[chunk][...].T

        total = jnp.dot(turned_ref[...], cols_ref[...], preferred_element_type=F32)
        out_ref[...] = (total * scale).astype(BF16)

    return pl.pallas_call(
        kernel,
        out_shape=jax.ShapeDtypeStruct(shape, BF16),
        grid=(cols.shape[1] // tile,),
        in_specs=specs,
        out_specs=pl.BlockSpec((block, tile), lambda j: (index, j)),
        scratch_shapes=[pltpu.VMEM((block, tokens), BF16)],
        input_output_aliases=aliases,
        cost_estimate=cost(
            4 * block * cols.size, 2 * cols.size + 2 * block * (tokens + cols.shape[1])
        ),
        compiler_params=pltpu.CompilerParams(vmem_limit_bytes=48 * MIB),
        name="hessian_rows",
    )(*ins)


def add_pieces(pieces, after):
    rows, rank = pieces[0].shape

    def kernel(*refs):
        total = refs[0][...].astype(F32)
        for ref in refs[1 : len(pieces)]:
            total += ref[...].astype(F32)
        refs[-1][...] = total

    return pl.pallas_call(
        kernel,
        out_shape=jax.ShapeDtypeStruct((rows, rank), F32),
        grid=(1,),
        in_specs=[pl.BlockSpec(memory_space=pltpu.VMEM)] * len(pieces)
        + [first_tile(after)],
        out_specs=pl.BlockSpec(memory_space=pltpu.VMEM),
        cost_estimate=cost(0, 12 * rows * rank),
        name="add_pieces",
    )(*pieces, after)


def pair_sum(values):
    while len(values) > 1:
        values = [values[i] + values[i + 1] for i in range(0, len(values), 2)]
    return values[0]


def body(activations, weight_tile, codes, group_scales, right_factor):
    wide_count = lax.axis_size("wide")
    narrow_count = lax.axis_size("narrow")
    wide_index = lax.axis_index("wide").astype(jnp.int32)
    narrow_index = lax.axis_index("narrow").astype(jnp.int32)
    tokens, features = activations.shape
    rows = weight_tile.shape[0]
    split = features // rows
    scale = 1.0 / (tokens * wide_count)

    cols = lax.all_gather(activations, "wide", axis=0, tiled=True)

    right_block = lax.dynamic_slice_in_dim(right_factor, narrow_index * features, features, 0)
    own = jnp.dot(activations, right_block, preferred_element_type=F32)
    residual = residual_tile(weight_tile, codes, group_scales)

    height = rows // CHUNKS
    chunks = []
    tail = [own]
    after = []
    for chunk in range(CHUNKS):
        mine = take_chunk(activations, chunk, height, split, tail, after)
        blocks, sources = exchange_blocks(mine, [] if chunk else [residual])
        chunks.append((blocks, sources))
        tail = []
        after = [blocks[near] for near, _ in sources if near] + [residual]

    where = narrow_index.reshape(1)
    y_blocks = sum_tails(*chunks[0], where, height)
    mask = 1
    while mask < wide_count:
        y_blocks = jnp.concatenate([y_blocks, flip(y_blocks, "wide", mask)], axis=0)
        mask *= 2

    row_chunks = []
    placed = []
    for chunk in range(CHUNKS):
        after = placed[-1:] if chunk else [y_blocks]
        every = place_blocks(*chunks[chunk], where, height, after)
        placed.append(every)
        every = every.reshape(narrow_count * split, tokens, height)
        chunk_rows = lax.all_to_all(every, "wide", split_axis=0, concat_axis=0, tiled=True)
        row_chunks.append(chunk_rows.reshape(tokens * wide_count, height))

    hr, gram = hr_and_gram(cols, y_blocks, wide_index.reshape(1), scale)
    partial = partial_product(residual, hr)
    share = rows // narrow_count
    received = []
    for m in range(narrow_count):
        piece = lax.dynamic_slice_in_dim(partial, (narrow_index ^ m) * share, share, 0)
        received.append(flip(piece, "narrow", m) if m else piece)

    hessian = None
    for chunk in range(CHUNKS):
        hessian = hessian_rows(
            [row_chunks[chunk]], cols, hessian, chunk, (rows, features), scale, [partial]
        )
    return add_pieces(received, hessian), gram, hessian


def solution(mesh):
    in_specs = (
        P("wide", "narrow"),
        P("wide", "narrow"),
        P("wide", "narrow"),
        P("wide", "narrow"),
        P(),
    )
    out_specs = (P(("wide", "narrow"), None), P(), P("wide", "narrow"))
    return jax.shard_map(body, mesh=mesh, in_specs=in_specs, out_specs=out_specs, check_vma=False)
```

```python
import functools

import jax
import jax.numpy as jnp
from jax import lax
from jax.experimental import pallas as pl
from jax.experimental.pallas import tpu as pltpu
from jax.sharding import PartitionSpec as P

CHUNKS = 2
MIB = 1024 * 1024
BF16 = jnp.bfloat16
F32 = jnp.float32


def flip(value, axis, mask):
    count = lax.axis_size(axis)
    return lax.ppermute(value, axis, [(i, i ^ mask) for i in range(count)])


def first_tile(value):
    shape = (1,) * (value.ndim - 2) + (16, 128)
    return pl.BlockSpec(shape, lambda *at: (0,) * value.ndim)


def cost(flops, moved):
    return pl.CostEstimate(flops=int(flops), bytes_accessed=int(moved), transcendentals=0)


def hr_and_gram(cols, y_blocks, where, scale):
    count, tokens, rank = y_blocks.shape
    features = cols.shape[1]
    tile = min(1024, features)

    def kernel(where_ref, cols_ref, y_ref, hr_ref, gram_ref, order_ref, turned_ref):
        @pl.when(pl.program_id(0) == 0)
        def _():
            for mask in range(count):
                at = pl.multiple_of((where_ref[0] ^ mask) * tokens, tokens)
                order_ref[pl.ds(at, tokens), :] = y_ref[mask]
            turned_ref[...] = order_ref[...].T
            gram = jnp.dot(turned_ref[...], order_ref[...], preferred_element_type=F32)
            gram_ref[...] = gram * scale

        total = jnp.dot(turned_ref[...], cols_ref[...], preferred_element_type=F32) * scale
        hr_ref[...] = total.T.astype(BF16)

    return pl.pallas_call(
        kernel,
        out_shape=(
            jax.ShapeDtypeStruct((features, rank), BF16),
            jax.ShapeDtypeStruct((rank, rank), F32),
        ),
        grid=(features // tile,),
        in_specs=[
            pl.BlockSpec(memory_space=pltpu.SMEM),
            pl.BlockSpec((count * tokens, tile), lambda j: (0, j)),
            pl.BlockSpec(y_blocks.shape, lambda j: (0, 0, 0)),
        ],
        out_specs=(
            pl.BlockSpec((tile, rank), lambda j: (j, 0)),
            pl.BlockSpec((rank, rank), lambda j: (0, 0)),
        ),
        scratch_shapes=[
            pltpu.VMEM((count * tokens, rank), BF16),
            pltpu.VMEM((rank, count * tokens), BF16),
        ],
        cost_estimate=cost(4 * count * tokens * features * rank, 4 * cols.size),
        compiler_params=pltpu.CompilerParams(vmem_limit_bytes=48 * MIB),
        name="hr_and_gram",
    )(where, cols, y_blocks)


def place_kernel(sources, where_ref, *refs):
    out_ref = refs[-1]
    count = len(sources)
    me = where_ref[0]
    for mask in range(count):
        other = me ^ mask
        near, far = sources[mask]

        def put(index, other=other):
            out_ref[other] = refs[index][:, :, : out_ref.shape[3]]

        if far is None:
            put(near)
        elif near is None:
            put(far)
        else:
            close = jnp.abs(me - other) <= count // 2
            pl.when(close)(functools.partial(put, near))
            pl.when(jnp.logical_not(close))(functools.partial(put, far))


def place_blocks(blocks, sources, where, height, after):
    count = len(sources)
    return pl.pallas_call(
        functools.partial(place_kernel, sources),
        out_shape=jax.ShapeDtypeStruct((count,) + blocks[0].shape[:2] + (height,), BF16),
        grid=(1,),
        in_specs=[pl.BlockSpec(memory_space=pltpu.SMEM)]
        + [pl.BlockSpec(memory_space=pltpu.VMEM)] * len(blocks)
        + [first_tile(value) for value in after],
        out_specs=pl.BlockSpec(memory_space=pltpu.VMEM),
        cost_estimate=cost(0, 4 * count * blocks[0].size),
        compiler_params=pltpu.CompilerParams(vmem_limit_bytes=48 * MIB),
        name="place_blocks",
    )(where, *blocks, *after)


def take_chunk(activations, chunk, height, split, tail, after):
    tokens, features = activations.shape
    rows = features // split
    share = tail[0].shape[1] // split if tail else 0

    def kernel(activations_ref, *refs):
        for s in range(split):
            at = s * rows + chunk * height
            refs[-1][s, :, :height] = activations_ref[:, at : at + height]
            if tail:
                refs[-1][s, :, height:] = refs[0][:, s * share : (s + 1) * share].astype(BF16)

    shape = (split, tokens, height + share)
    return pl.pallas_call(
        kernel,
        out_shape=jax.ShapeDtypeStruct(shape, BF16),
        grid=(1,),
        in_specs=[pl.BlockSpec((tokens, features), lambda i: (0, 0))]
        + [pl.BlockSpec(value.shape, lambda i: (0, 0)) for value in tail]
        + [first_tile(value) for value in after],
        out_specs=pl.BlockSpec(shape, lambda i: (0, 0, 0)),
        cost_estimate=cost(0, 4 * split * tokens * height),
        name="take_chunk",
    )(activations, *tail, *after)


def sum_tails(blocks, sources, where, height, after):
    split, tokens, width = blocks[0].shape
    share = width - height
    count = len(sources)
    spec = pl.BlockSpec((split, tokens, share), lambda i: (0, 0, height // share))

    def kernel(where_ref, *refs):
        out_ref, held_ref = refs[-2:]
        me = where_ref[0]
        for mask in range(count):
            near, far = sources[mask]

            def put(index, mask=mask):
                held_ref[mask] = refs[index][...].astype(F32)

            if far is None:
                put(near)
            elif near is None:
                put(far)
            else:
                close = jnp.abs(me - (me ^ mask)) <= count // 2
                pl.when(close)(functools.partial(put, near))
                pl.when(jnp.logical_not(close))(functools.partial(put, far))
        total = pair_sum([held_ref[mask] for mask in range(count)])
        for s in range(split):
            out_ref[0, :, s * share : (s + 1) * share] = total[s].astype(BF16)

    return pl.pallas_call(
        kernel,
        out_shape=jax.ShapeDtypeStruct((1, tokens, split * share), BF16),
        grid=(1,),
        in_specs=[pl.BlockSpec(memory_space=pltpu.SMEM)]
        + [spec] * len(blocks)
        + [first_tile(value) for value in after],
        out_specs=pl.BlockSpec((1, tokens, split * share), lambda i: (0, 0, 0)),
        scratch_shapes=[pltpu.VMEM((count, split, tokens, share), F32)],
        cost_estimate=cost(0, 4 * count * split * tokens * share),
        name="sum_tails",
    )(where, *blocks, *after)


def relay(value, after):
    def kernel(value_ref, *refs):
        refs[-1][...] = value_ref[...]

    spec = pl.BlockSpec(value.shape, lambda i: (0, 0, 0))
    return pl.pallas_call(
        kernel,
        out_shape=jax.ShapeDtypeStruct(value.shape, value.dtype),
        grid=(1,),
        in_specs=[spec] + [first_tile(other) for other in after],
        out_specs=spec,
        cost_estimate=cost(0, 4 * value.size),
        name="relay",
    )(value, *after)


def exchange_blocks(mine, after):
    count = lax.axis_size("narrow")
    half = count // 2
    blocks = [mine]
    sources = [(0, None)]
    direct = {}
    order = sorted(range(1, count), key=lambda m: (m != half, m))
    for mask in order:
        pairs = [(i, i ^ mask) for i in range(count) if abs(i - (i ^ mask)) <= half]
        direct[mask] = lax.ppermute(mine, "narrow", pairs) if pairs else None
    onward = direct.get(half)
    if after and count > 2:
        onward = relay(onward, after)
    for mask in range(1, count):
        near = far = None
        if direct[mask] is not None:
            near = len(blocks)
            blocks.append(direct[mask])
        pairs = [(i ^ half, i ^ mask) for i in range(count) if abs(i - (i ^ mask)) > half]
        if pairs:
            far = len(blocks)
            blocks.append(lax.ppermute(onward, "narrow", pairs))
        sources.append((near, far))
    return blocks, sources


def residual_kernel(weight_ref, codes_ref, scales_ref, out_ref):
    groups = scales_ref.shape[1]
    width = weight_ref.shape[1] // groups
    scales = scales_ref[...]
    parts = []
    for group in range(groups):
        at = slice(group * width, (group + 1) * width)
        quantized = codes_ref[:, at].astype(F32) * scales[:, group : group + 1]
        parts.append((weight_ref[:, at].astype(F32) - quantized).astype(BF16))
    out_ref[...] = jnp.concatenate(parts, axis=1)


def residual_tile(weight, codes, scales):
    rows, features = weight.shape
    block = min(256, rows)
    return pl.pallas_call(
        residual_kernel,
        out_shape=jax.ShapeDtypeStruct((rows, features), BF16),
        grid=(rows // block,),
        in_specs=[
            pl.BlockSpec((block, features), lambda i: (i, 0)),
            pl.BlockSpec((block, features), lambda i: (i, 0)),
            pl.BlockSpec((block, scales.shape[1]), lambda i: (i, 0)),
        ],
        out_specs=pl.BlockSpec((block, features), lambda i: (i, 0)),
        compiler_params=pltpu.CompilerParams(vmem_limit_bytes=48 * MIB),
        cost_estimate=cost(0, 11 * rows * features),
        name="residual_tile",
    )(weight, codes, scales)


def product_kernel(residual_ref, hr_ref, out_ref):
    out_ref[...] = jnp.dot(residual_ref[...], hr_ref[...], preferred_element_type=F32).astype(BF16)


def partial_product(residual, hr):
    rows, features = residual.shape
    rank = hr.shape[1]
    block = min(512, rows)
    return pl.pallas_call(
        product_kernel,
        out_shape=jax.ShapeDtypeStruct((rows, rank), BF16),
        grid=(rows // block,),
        in_specs=[
            pl.BlockSpec((block, features), lambda i: (i, 0)),
            pl.BlockSpec((features, rank), lambda i: (0, 0)),
        ],
        out_specs=pl.BlockSpec((block, rank), lambda i: (i, 0)),
        compiler_params=pltpu.CompilerParams(vmem_limit_bytes=48 * MIB),
        cost_estimate=cost(4 * rows * features * rank, 3 * rows * features),
        name="partial_product",
    )(residual, hr)


def hessian_rows(row_chunks, cols, earlier, index, shape, scale, after):
    tokens, height = row_chunks[0].shape
    block = height * len(row_chunks)
    tile = min(1024, cols.shape[1])
    count = len(row_chunks)
    ins = [*row_chunks, cols]
    specs = [pl.BlockSpec((tokens, height), lambda j: (0, 0))] * count
    specs.append(pl.BlockSpec((tokens, tile), lambda j: (0, j)))
    aliases = {}
    if earlier is not None:
        aliases = {len(ins): 0}
        ins.append(earlier)
        specs.append(pl.BlockSpec(memory_space=pl.ANY))
    for value in after:
        ins.append(value)
        specs.append(first_tile(value))

    def kernel(*refs):
        cols_ref = refs[count]
        out_ref, turned_ref = refs[-2:]

        @pl.when(pl.program_id(0) == 0)
        def _():
            for chunk in range(count):
                turned_ref[chunk * height : (chunk + 1) * height] = refs[chunk][...].T

        total = jnp.dot(turned_ref[...], cols_ref[...], preferred_element_type=F32)
        out_ref[...] = (total * scale).astype(BF16)

    return pl.pallas_call(
        kernel,
        out_shape=jax.ShapeDtypeStruct(shape, BF16),
        grid=(cols.shape[1] // tile,),
        in_specs=specs,
        out_specs=pl.BlockSpec((block, tile), lambda j: (index, j)),
        scratch_shapes=[pltpu.VMEM((block, tokens), BF16)],
        input_output_aliases=aliases,
        cost_estimate=cost(
            4 * block * cols.size, 2 * cols.size + 2 * block * (tokens + cols.shape[1])
        ),
        compiler_params=pltpu.CompilerParams(vmem_limit_bytes=48 * MIB),
        name="hessian_rows",
    )(*ins)


def add_pieces(pieces, after):
    rows, rank = pieces[0].shape

    def kernel(*refs):
        total = refs[0][...].astype(F32)
        for ref in refs[1 : len(pieces)]:
            total += ref[...].astype(F32)
        refs[-1][...] = total

    return pl.pallas_call(
        kernel,
        out_shape=jax.ShapeDtypeStruct((rows, rank), F32),
        grid=(1,),
        in_specs=[pl.BlockSpec(memory_space=pltpu.VMEM)] * len(pieces)
        + [first_tile(after)],
        out_specs=pl.BlockSpec(memory_space=pltpu.VMEM),
        cost_estimate=cost(0, 12 * rows * rank),
        name="add_pieces",
    )(*pieces, after)


def pair_sum(values):
    while len(values) > 1:
        values = [values[i] + values[i + 1] for i in range(0, len(values), 2)]
    return values[0]


def body(activations, weight_tile, codes, group_scales, right_factor):
    wide_count = lax.axis_size("wide")
    narrow_count = lax.axis_size("narrow")
    wide_index = lax.axis_index("wide").astype(jnp.int32)
    narrow_index = lax.axis_index("narrow").astype(jnp.int32)
    tokens, features = activations.shape
    rows = weight_tile.shape[0]
    split = features // rows
    scale = 1.0 / (tokens * wide_count)

    cols = lax.all_gather(activations, "wide", axis=0, tiled=True)

    right_block = lax.dynamic_slice_in_dim(right_factor, narrow_index * features, features, 0)
    own = jnp.dot(activations, right_block, preferred_element_type=F32)
    residual = residual_tile(weight_tile, codes, group_scales)

    height = rows // CHUNKS
    chunks = []
    tail = [own]
    after = []
    for chunk in range(CHUNKS):
        mine = take_chunk(activations, chunk, height, split, tail, after)
        blocks, sources = exchange_blocks(mine, [] if chunk else [residual])
        chunks.append((blocks, sources))
        tail = []
        after = [blocks[near] for near, _ in sources if near] + [residual]

    where = narrow_index.reshape(1)
    y_blocks = sum_tails(*chunks[0], where, height, [blocks[0] for blocks, _ in chunks[1:]])
    mask = 1
    while mask < wide_count:
        y_blocks = jnp.concatenate([y_blocks, flip(y_blocks, "wide", mask)], axis=0)
        mask *= 2

    hr, gram = hr_and_gram(cols, y_blocks, wide_index.reshape(1), scale)

    row_chunks = []
    placed = []
    for chunk in range(CHUNKS):
        after = placed[-1:] + [hr] if chunk else [y_blocks]
        every = place_blocks(*chunks[chunk], where, height, after)
        placed.append(every)
        every = every.reshape(narrow_count * split, tokens, height)
        chunk_rows = lax.all_to_all(every, "wide", split_axis=0, concat_axis=0, tiled=True)
        row_chunks.append(chunk_rows.reshape(tokens * wide_count, height))

    partial = partial_product(residual, hr)
    share = rows // narrow_count
    received = []
    for m in range(narrow_count):
        piece = lax.dynamic_slice_in_dim(partial, (narrow_index ^ m) * share, share, 0)
        received.append(flip(piece, "narrow", m) if m else piece)

    hessian = None
    for chunk in range(CHUNKS):
        hessian = hessian_rows(
            [row_chunks[chunk]], cols, hessian, chunk, (rows, features), scale, [partial]
        )
    return add_pieces(received, hessian), gram, hessian


def solution(mesh):
    in_specs = (
        P("wide", "narrow"),
        P("wide", "narrow"),
        P("wide", "narrow"),
        P("wide", "narrow"),
        P(),
    )
    out_specs = (P(("wide", "narrow"), None), P(), P("wide", "narrow"))
    return jax.shard_map(body, mesh=mesh, in_specs=in_specs, out_specs=out_specs, check_vma=False)
```

```python
import functools

import jax
import jax.numpy as jnp
from jax import lax
from jax.experimental import pallas as pl
from jax.experimental.pallas import tpu as pltpu
from jax.sharding import PartitionSpec as P

CHUNKS = 2
MIB = 1024 * 1024
BF16 = jnp.bfloat16
F32 = jnp.float32


def flip(value, axis, mask):
    count = lax.axis_size(axis)
    return lax.ppermute(value, axis, [(i, i ^ mask) for i in range(count)])


def first_tile(value):
    shape = (1,) * (value.ndim - 2) + (16, 128)
    return pl.BlockSpec(shape, lambda *at: (0,) * value.ndim)


def cost(flops, moved):
    return pl.CostEstimate(flops=int(flops), bytes_accessed=int(moved), transcendentals=0)


def hr_and_gram(cols, y_blocks, where, scale):
    count, tokens, rank = y_blocks.shape
    features = cols.shape[1]
    tile = min(1024, features)

    def kernel(where_ref, cols_ref, y_ref, hr_ref, gram_ref, order_ref, turned_ref):
        @pl.when(pl.program_id(0) == 0)
        def _():
            for mask in range(count):
                at = pl.multiple_of((where_ref[0] ^ mask) * tokens, tokens)
                order_ref[pl.ds(at, tokens), :] = y_ref[mask]
            turned_ref[...] = order_ref[...].T
            gram = jnp.dot(turned_ref[...], order_ref[...], preferred_element_type=F32)
            gram_ref[...] = gram * scale

        total = jnp.dot(turned_ref[...], cols_ref[...], preferred_element_type=F32) * scale
        hr_ref[...] = total.T.astype(BF16)

    return pl.pallas_call(
        kernel,
        out_shape=(
            jax.ShapeDtypeStruct((features, rank), BF16),
            jax.ShapeDtypeStruct((rank, rank), F32),
        ),
        grid=(features // tile,),
        in_specs=[
            pl.BlockSpec(memory_space=pltpu.SMEM),
            pl.BlockSpec((count * tokens, tile), lambda j: (0, j)),
            pl.BlockSpec(y_blocks.shape, lambda j: (0, 0, 0)),
        ],
        out_specs=(
            pl.BlockSpec((tile, rank), lambda j: (j, 0)),
            pl.BlockSpec((rank, rank), lambda j: (0, 0)),
        ),
        scratch_shapes=[
            pltpu.VMEM((count * tokens, rank), BF16),
            pltpu.VMEM((rank, count * tokens), BF16),
        ],
        cost_estimate=cost(4 * count * tokens * features * rank, 4 * cols.size),
        compiler_params=pltpu.CompilerParams(vmem_limit_bytes=48 * MIB),
        name="hr_and_gram",
    )(where, cols, y_blocks)


def place_kernel(sources, where_ref, *refs):
    out_ref = refs[-1]
    count = len(sources)
    me = where_ref[0]
    for mask in range(count):
        other = me ^ mask
        near, far = sources[mask]

        def put(index, other=other):
            out_ref[other] = refs[index][:, :, : out_ref.shape[3]]

        if far is None:
            put(near)
        elif near is None:
            put(far)
        else:
            close = jnp.abs(me - other) <= count // 2
            pl.when(close)(functools.partial(put, near))
            pl.when(jnp.logical_not(close))(functools.partial(put, far))


def place_blocks(blocks, sources, where, height, after):
    count = len(sources)
    return pl.pallas_call(
        functools.partial(place_kernel, sources),
        out_shape=jax.ShapeDtypeStruct((count,) + blocks[0].shape[:2] + (height,), BF16),
        grid=(1,),
        in_specs=[pl.BlockSpec(memory_space=pltpu.SMEM)]
        + [pl.BlockSpec(memory_space=pltpu.VMEM)] * len(blocks)
        + [first_tile(value) for value in after],
        out_specs=pl.BlockSpec(memory_space=pltpu.VMEM),
        cost_estimate=cost(0, 4 * count * blocks[0].size),
        compiler_params=pltpu.CompilerParams(vmem_limit_bytes=48 * MIB),
        name="place_blocks",
    )(where, *blocks, *after)


def take_chunk(activations, chunk, height, split, tail, after):
    tokens, features = activations.shape
    rows = features // split
    share = tail[0].shape[1] // split if tail else 0

    def kernel(activations_ref, *refs):
        for s in range(split):
            at = s * rows + chunk * height
            refs[-1][s, :, :height] = activations_ref[:, at : at + height]
            if tail:
                refs[-1][s, :, height:] = refs[0][:, s * share : (s + 1) * share].astype(BF16)

    shape = (split, tokens, height + share)
    return pl.pallas_call(
        kernel,
        out_shape=jax.ShapeDtypeStruct(shape, BF16),
        grid=(1,),
        in_specs=[pl.BlockSpec((tokens, features), lambda i: (0, 0))]
        + [pl.BlockSpec(value.shape, lambda i: (0, 0)) for value in tail]
        + [first_tile(value) for value in after],
        out_specs=pl.BlockSpec(shape, lambda i: (0, 0, 0)),
        cost_estimate=cost(0, 4 * split * tokens * height),
        name="take_chunk",
    )(activations, *tail, *after)


def sum_tails(blocks, sources, where, height, after):
    split, tokens, width = blocks[0].shape
    share = width - height
    count = len(sources)
    spec = pl.BlockSpec((split, tokens, share), lambda i: (0, 0, height // share))

    def kernel(where_ref, *refs):
        out_ref, held_ref = refs[-2:]
        me = where_ref[0]
        for mask in range(count):
            near, far = sources[mask]

            def put(index, mask=mask):
                held_ref[mask] = refs[index][...].astype(F32)

            if far is None:
                put(near)
            elif near is None:
                put(far)
            else:
                close = jnp.abs(me - (me ^ mask)) <= count // 2
                pl.when(close)(functools.partial(put, near))
                pl.when(jnp.logical_not(close))(functools.partial(put, far))
        total = pair_sum([held_ref[mask] for mask in range(count)])
        for s in range(split):
            out_ref[0, :, s * share : (s + 1) * share] = total[s].astype(BF16)

    return pl.pallas_call(
        kernel,
        out_shape=jax.ShapeDtypeStruct((1, tokens, split * share), BF16),
        grid=(1,),
        in_specs=[pl.BlockSpec(memory_space=pltpu.SMEM)]
        + [spec] * len(blocks)
        + [first_tile(value) for value in after],
        out_specs=pl.BlockSpec((1, tokens, split * share), lambda i: (0, 0, 0)),
        scratch_shapes=[pltpu.VMEM((count, split, tokens, share), F32)],
        cost_estimate=cost(0, 4 * count * split * tokens * share),
        name="sum_tails",
    )(where, *blocks, *after)


def relay(value, after):
    def kernel(value_ref, *refs):
        refs[-1][...] = value_ref[...]

    spec = pl.BlockSpec(value.shape, lambda i: (0, 0, 0))
    return pl.pallas_call(
        kernel,
        out_shape=jax.ShapeDtypeStruct(value.shape, value.dtype),
        grid=(1,),
        in_specs=[spec] + [first_tile(other) for other in after],
        out_specs=spec,
        cost_estimate=cost(0, 4 * value.size),
        name="relay",
    )(value, *after)


def exchange_blocks(mine, after):
    count = lax.axis_size("narrow")
    half = count // 2
    blocks = [mine]
    sources = [(0, None)]
    direct = {}
    order = sorted(range(1, count), key=lambda m: (m != half, m))
    for mask in order:
        pairs = [(i, i ^ mask) for i in range(count) if abs(i - (i ^ mask)) <= half]
        direct[mask] = lax.ppermute(mine, "narrow", pairs) if pairs else None
    onward = direct.get(half)
    if after and count > 2:
        onward = relay(onward, after)
    for mask in range(1, count):
        near = far = None
        if direct[mask] is not None:
            near = len(blocks)
            blocks.append(direct[mask])
        pairs = [(i ^ half, i ^ mask) for i in range(count) if abs(i - (i ^ mask)) > half]
        if pairs:
            far = len(blocks)
            blocks.append(lax.ppermute(onward, "narrow", pairs))
        sources.append((near, far))
    return blocks, sources


def residual_kernel(weight_ref, codes_ref, scales_ref, out_ref):
    groups = scales_ref.shape[1]
    width = weight_ref.shape[1] // groups
    scales = scales_ref[...]
    parts = []
    for group in range(groups):
        at = slice(group * width, (group + 1) * width)
        quantized = codes_ref[:, at].astype(F32) * scales[:, group : group + 1]
        parts.append((weight_ref[:, at].astype(F32) - quantized).astype(BF16))
    out_ref[...] = jnp.concatenate(parts, axis=1)


def residual_tile(weight, codes, scales):
    rows, features = weight.shape
    block = min(256, rows)
    return pl.pallas_call(
        residual_kernel,
        out_shape=jax.ShapeDtypeStruct((rows, features), BF16),
        grid=(rows // block,),
        in_specs=[
            pl.BlockSpec((block, features), lambda i: (i, 0)),
            pl.BlockSpec((block, features), lambda i: (i, 0)),
            pl.BlockSpec((block, scales.shape[1]), lambda i: (i, 0)),
        ],
        out_specs=pl.BlockSpec((block, features), lambda i: (i, 0)),
        compiler_params=pltpu.CompilerParams(vmem_limit_bytes=48 * MIB),
        cost_estimate=cost(0, 11 * rows * features),
        name="residual_tile",
    )(weight, codes, scales)


def product_kernel(residual_ref, hr_ref, out_ref):
    out_ref[...] = jnp.dot(residual_ref[...], hr_ref[...], preferred_element_type=F32).astype(BF16)


def partial_product(residual, hr):
    rows, features = residual.shape
    rank = hr.shape[1]
    block = min(512, rows)
    return pl.pallas_call(
        product_kernel,
        out_shape=jax.ShapeDtypeStruct((rows, rank), BF16),
        grid=(rows // block,),
        in_specs=[
            pl.BlockSpec((block, features), lambda i: (i, 0)),
            pl.BlockSpec((features, rank), lambda i: (0, 0)),
        ],
        out_specs=pl.BlockSpec((block, rank), lambda i: (i, 0)),
        compiler_params=pltpu.CompilerParams(vmem_limit_bytes=48 * MIB),
        cost_estimate=cost(4 * rows * features * rank, 3 * rows * features),
        name="partial_product",
    )(residual, hr)


def hessian_rows(row_chunks, cols, earlier, index, shape, scale, after):
    tokens, height = row_chunks[0].shape
    block = height * len(row_chunks)
    tile = min(1024, cols.shape[1])
    count = len(row_chunks)
    ins = [*row_chunks, cols]
    specs = [pl.BlockSpec((tokens, height), lambda j: (0, 0))] * count
    specs.append(pl.BlockSpec((tokens, tile), lambda j: (0, j)))
    aliases = {}
    if earlier is not None:
        aliases = {len(ins): 0}
        ins.append(earlier)
        specs.append(pl.BlockSpec(memory_space=pl.ANY))
    for value in after:
        ins.append(value)
        specs.append(first_tile(value))

    def kernel(*refs):
        cols_ref = refs[count]
        out_ref, turned_ref = refs[-2:]

        @pl.when(pl.program_id(0) == 0)
        def _():
            for chunk in range(count):
                turned_ref[chunk * height : (chunk + 1) * height] = refs[chunk][...].T

        total = jnp.dot(turned_ref[...], cols_ref[...], preferred_element_type=F32)
        out_ref[...] = (total * scale).astype(BF16)

    return pl.pallas_call(
        kernel,
        out_shape=jax.ShapeDtypeStruct(shape, BF16),
        grid=(cols.shape[1] // tile,),
        in_specs=specs,
        out_specs=pl.BlockSpec((block, tile), lambda j: (index, j)),
        scratch_shapes=[pltpu.VMEM((block, tokens), BF16)],
        input_output_aliases=aliases,
        cost_estimate=cost(
            4 * block * cols.size, 2 * cols.size + 2 * block * (tokens + cols.shape[1])
        ),
        compiler_params=pltpu.CompilerParams(vmem_limit_bytes=48 * MIB),
        name="hessian_rows",
    )(*ins)


def add_pieces(pieces, after):
    rows, rank = pieces[0].shape

    def kernel(*refs):
        total = refs[0][...].astype(F32)
        for ref in refs[1 : len(pieces)]:
            total += ref[...].astype(F32)
        refs[-1][...] = total

    return pl.pallas_call(
        kernel,
        out_shape=jax.ShapeDtypeStruct((rows, rank), F32),
        grid=(1,),
        in_specs=[pl.BlockSpec(memory_space=pltpu.VMEM)] * len(pieces)
        + [first_tile(after)],
        out_specs=pl.BlockSpec(memory_space=pltpu.VMEM),
        cost_estimate=cost(0, 12 * rows * rank),
        name="add_pieces",
    )(*pieces, after)


def pair_sum(values):
    while len(values) > 1:
        values = [values[i] + values[i + 1] for i in range(0, len(values), 2)]
    return values[0]


def body(activations, weight_tile, codes, group_scales, right_factor):
    wide_count = lax.axis_size("wide")
    narrow_count = lax.axis_size("narrow")
    wide_index = lax.axis_index("wide").astype(jnp.int32)
    narrow_index = lax.axis_index("narrow").astype(jnp.int32)
    tokens, features = activations.shape
    rows = weight_tile.shape[0]
    split = features // rows
    scale = 1.0 / (tokens * wide_count)

    cols = lax.all_gather(activations, "wide", axis=0, tiled=True)

    right_block = lax.dynamic_slice_in_dim(right_factor, narrow_index * features, features, 0)
    own = jnp.dot(activations, right_block, preferred_element_type=F32)
    residual = residual_tile(weight_tile, codes, group_scales)

    height = rows // CHUNKS
    chunks = []
    tail = [own]
    after = []
    for chunk in range(CHUNKS):
        mine = take_chunk(activations, chunk, height, split, tail, after)
        blocks, sources = exchange_blocks(mine, [] if chunk else [residual])
        chunks.append((blocks, sources))
        tail = []
        after = [blocks[near] for near, _ in sources if near] + [residual]

    where = narrow_index.reshape(1)
    later, later_at = chunks[1]
    direct = [later[near] for near, _ in later_at if near]
    y_blocks = sum_tails(*chunks[0], where, height, [later[0]] + direct[-1:])
    mask = 1
    while mask < wide_count:
        sent = y_blocks
        if 2 * mask == wide_count:
            sent = relay(y_blocks, [later[later_at[narrow_count // 2][0]]])
        y_blocks = jnp.concatenate([sent, flip(sent, "wide", mask)], axis=0)
        mask *= 2

    hr, gram = hr_and_gram(cols, y_blocks, wide_index.reshape(1), scale)

    row_chunks = []
    placed = []
    for chunk in range(CHUNKS):
        after = placed[-1:] + [hr] if chunk else [y_blocks] + direct
        every = place_blocks(*chunks[chunk], where, height, after)
        placed.append(every)
        every = every.reshape(narrow_count * split, tokens, height)
        chunk_rows = lax.all_to_all(every, "wide", split_axis=0, concat_axis=0, tiled=True)
        row_chunks.append(chunk_rows.reshape(tokens * wide_count, height))

    partial = partial_product(residual, hr)
    share = rows // narrow_count
    received = []
    for m in range(narrow_count):
        piece = lax.dynamic_slice_in_dim(partial, (narrow_index ^ m) * share, share, 0)
        received.append(flip(piece, "narrow", m) if m else piece)

    hessian = None
    for chunk in range(CHUNKS):
        hessian = hessian_rows(
            [row_chunks[chunk]], cols, hessian, chunk, (rows, features), scale, [partial]
        )
    return add_pieces(received, hessian), gram, hessian


def solution(mesh):
    in_specs = (
        P("wide", "narrow"),
        P("wide", "narrow"),
        P("wide", "narrow"),
        P("wide", "narrow"),
        P(),
    )
    out_specs = (P(("wide", "narrow"), None), P(), P("wide", "narrow"))
    return jax.shard_map(body, mesh=mesh, in_specs=in_specs, out_specs=out_specs, check_vma=False)
```

```python
import functools

import jax
import jax.numpy as jnp
from jax import lax
from jax.experimental import pallas as pl
from jax.experimental.pallas import tpu as pltpu
from jax.sharding import PartitionSpec as P

CHUNKS = 2
MIB = 1024 * 1024
BF16 = jnp.bfloat16
F32 = jnp.float32


def flip(value, axis, mask):
    count = lax.axis_size(axis)
    return lax.ppermute(value, axis, [(i, i ^ mask) for i in range(count)])


def first_tile(value):
    shape = (1,) * (value.ndim - 2) + (16, 128)
    return pl.BlockSpec(shape, lambda *at: (0,) * value.ndim)


def cost(flops, moved):
    return pl.CostEstimate(flops=int(flops), bytes_accessed=int(moved), transcendentals=0)


def hr_and_gram(cols, y, scale):
    tokens, rank = y.shape
    features = cols.shape[1]
    tile = min(1024, features)

    def kernel(cols_ref, y_ref, hr_ref, gram_ref, turned_ref):
        @pl.when(pl.program_id(0) == 0)
        def _():
            turned_ref[...] = y_ref[...].T
            gram = jnp.dot(turned_ref[...], y_ref[...], preferred_element_type=F32)
            gram_ref[...] = gram * scale

        total = jnp.dot(turned_ref[...], cols_ref[...], preferred_element_type=F32) * scale
        hr_ref[...] = total.T.astype(BF16)

    return pl.pallas_call(
        kernel,
        out_shape=(
            jax.ShapeDtypeStruct((features, rank), BF16),
            jax.ShapeDtypeStruct((rank, rank), F32),
        ),
        grid=(features // tile,),
        in_specs=[
            pl.BlockSpec((tokens, tile), lambda j: (0, j)),
            pl.BlockSpec((tokens, rank), lambda j: (0, 0)),
        ],
        out_specs=(
            pl.BlockSpec((tile, rank), lambda j: (j, 0)),
            pl.BlockSpec((rank, rank), lambda j: (0, 0)),
        ),
        scratch_shapes=[pltpu.VMEM((rank, tokens), BF16)],
        cost_estimate=cost(4 * tokens * features * rank, 4 * cols.size),
        compiler_params=pltpu.CompilerParams(vmem_limit_bytes=48 * MIB),
        name="hr_and_gram",
    )(cols, y)


def place_kernel(sources, where_ref, *refs):
    out_ref = refs[-1]
    count = len(sources)
    me = where_ref[0]
    for mask in range(count):
        other = me ^ mask
        near, far = sources[mask]

        def put(index, other=other):
            out_ref[other] = refs[index][:, :, : out_ref.shape[3]]

        if far is None:
            put(near)
        elif near is None:
            put(far)
        else:
            close = jnp.abs(me - other) <= count // 2
            pl.when(close)(functools.partial(put, near))
            pl.when(jnp.logical_not(close))(functools.partial(put, far))


def place_blocks(blocks, sources, where, height, after):
    count = len(sources)
    return pl.pallas_call(
        functools.partial(place_kernel, sources),
        out_shape=jax.ShapeDtypeStruct((count,) + blocks[0].shape[:2] + (height,), BF16),
        grid=(1,),
        in_specs=[pl.BlockSpec(memory_space=pltpu.SMEM)]
        + [pl.BlockSpec(memory_space=pltpu.VMEM)] * len(blocks)
        + [first_tile(value) for value in after],
        out_specs=pl.BlockSpec(memory_space=pltpu.VMEM),
        cost_estimate=cost(0, 4 * count * blocks[0].size),
        compiler_params=pltpu.CompilerParams(vmem_limit_bytes=48 * MIB),
        name="place_blocks",
    )(where, *blocks, *after)


def take_chunk(activations, chunk, height, split, tail, after):
    tokens, features = activations.shape
    rows = features // split
    share = tail[0].shape[1] // split if tail else 0

    def kernel(activations_ref, *refs):
        for s in range(split):
            at = s * rows + chunk * height
            refs[-1][s, :, :height] = activations_ref[:, at : at + height]
            if tail:
                refs[-1][s, :, height:] = refs[0][:, s * share : (s + 1) * share].astype(BF16)

    shape = (split, tokens, height + share)
    return pl.pallas_call(
        kernel,
        out_shape=jax.ShapeDtypeStruct(shape, BF16),
        grid=(1,),
        in_specs=[pl.BlockSpec((tokens, features), lambda i: (0, 0))]
        + [pl.BlockSpec(value.shape, lambda i: (0, 0)) for value in tail]
        + [first_tile(value) for value in after],
        out_specs=pl.BlockSpec(shape, lambda i: (0, 0, 0)),
        cost_estimate=cost(0, 4 * split * tokens * height),
        name="take_chunk",
    )(activations, *tail, *after)


def sum_tails(blocks, sources, where, height, after):
    split, tokens, width = blocks[0].shape
    share = width - height
    count = len(sources)
    spec = pl.BlockSpec((split, tokens, share), lambda i: (0, 0, height // share))

    def kernel(where_ref, *refs):
        out_ref, held_ref = refs[-2:]
        me = where_ref[0]
        for mask in range(count):
            near, far = sources[mask]

            def put(index, mask=mask):
                held_ref[mask] = refs[index][...].astype(F32)

            if far is None:
                put(near)
            elif near is None:
                put(far)
            else:
                close = jnp.abs(me - (me ^ mask)) <= count // 2
                pl.when(close)(functools.partial(put, near))
                pl.when(jnp.logical_not(close))(functools.partial(put, far))
        total = pair_sum([held_ref[mask] for mask in range(count)])
        for s in range(split):
            out_ref[0, :, s * share : (s + 1) * share] = total[s].astype(BF16)

    return pl.pallas_call(
        kernel,
        out_shape=jax.ShapeDtypeStruct((1, tokens, split * share), BF16),
        grid=(1,),
        in_specs=[pl.BlockSpec(memory_space=pltpu.SMEM)]
        + [spec] * len(blocks)
        + [first_tile(value) for value in after],
        out_specs=pl.BlockSpec((1, tokens, split * share), lambda i: (0, 0, 0)),
        scratch_shapes=[pltpu.VMEM((count, split, tokens, share), F32)],
        cost_estimate=cost(0, 4 * count * split * tokens * share),
        name="sum_tails",
    )(where, *blocks, *after)


def relay(value, after):
    def kernel(value_ref, *refs):
        refs[-1][...] = value_ref[...]

    spec = pl.BlockSpec(value.shape, lambda i: (0, 0, 0))
    return pl.pallas_call(
        kernel,
        out_shape=jax.ShapeDtypeStruct(value.shape, value.dtype),
        grid=(1,),
        in_specs=[spec] + [first_tile(other) for other in after],
        out_specs=spec,
        cost_estimate=cost(0, 4 * value.size),
        name="relay",
    )(value, *after)


def exchange_blocks(mine, after):
    count = lax.axis_size("narrow")
    half = count // 2
    blocks = [mine]
    sources = [(0, None)]
    direct = {}
    order = sorted(range(1, count), key=lambda m: (m != half, m))
    for mask in order:
        pairs = [(i, i ^ mask) for i in range(count) if abs(i - (i ^ mask)) <= half]
        direct[mask] = lax.ppermute(mine, "narrow", pairs) if pairs else None
    onward = direct.get(half)
    if after and count > 2:
        onward = relay(onward, after)
    for mask in range(1, count):
        near = far = None
        if direct[mask] is not None:
            near = len(blocks)
            blocks.append(direct[mask])
        pairs = [(i ^ half, i ^ mask) for i in range(count) if abs(i - (i ^ mask)) > half]
        if pairs:
            far = len(blocks)
            blocks.append(lax.ppermute(onward, "narrow", pairs))
        sources.append((near, far))
    return blocks, sources


def residual_kernel(weight_ref, codes_ref, scales_ref, out_ref):
    groups = scales_ref.shape[1]
    width = weight_ref.shape[1] // groups
    scales = scales_ref[...]
    parts = []
    for group in range(groups):
        at = slice(group * width, (group + 1) * width)
        quantized = codes_ref[:, at].astype(F32) * scales[:, group : group + 1]
        parts.append((weight_ref[:, at].astype(F32) - quantized).astype(BF16))
    out_ref[...] = jnp.concatenate(parts, axis=1)


def residual_tile(weight, codes, scales):
    rows, features = weight.shape
    block = min(256, rows)
    return pl.pallas_call(
        residual_kernel,
        out_shape=jax.ShapeDtypeStruct((rows, features), BF16),
        grid=(rows // block,),
        in_specs=[
            pl.BlockSpec((block, features), lambda i: (i, 0)),
            pl.BlockSpec((block, features), lambda i: (i, 0)),
            pl.BlockSpec((block, scales.shape[1]), lambda i: (i, 0)),
        ],
        out_specs=pl.BlockSpec((block, features), lambda i: (i, 0)),
        compiler_params=pltpu.CompilerParams(vmem_limit_bytes=48 * MIB),
        cost_estimate=cost(0, 11 * rows * features),
        name="residual_tile",
    )(weight, codes, scales)


def product_kernel(residual_ref, hr_ref, out_ref):
    out_ref[...] = jnp.dot(residual_ref[...], hr_ref[...], preferred_element_type=F32).astype(BF16)


def partial_product(residual, hr):
    rows, features = residual.shape
    rank = hr.shape[1]
    block = min(512, rows)
    return pl.pallas_call(
        product_kernel,
        out_shape=jax.ShapeDtypeStruct((rows, rank), BF16),
        grid=(rows // block,),
        in_specs=[
            pl.BlockSpec((block, features), lambda i: (i, 0)),
            pl.BlockSpec((features, rank), lambda i: (0, 0)),
        ],
        out_specs=pl.BlockSpec((block, rank), lambda i: (i, 0)),
        compiler_params=pltpu.CompilerParams(vmem_limit_bytes=48 * MIB),
        cost_estimate=cost(4 * rows * features * rank, 3 * rows * features),
        name="partial_product",
    )(residual, hr)


def hessian_rows(row_chunks, cols, earlier, index, shape, scale, after):
    tokens, height = row_chunks[0].shape
    block = height * len(row_chunks)
    tile = min(1024, cols.shape[1])
    count = len(row_chunks)
    ins = [*row_chunks, cols]
    specs = [pl.BlockSpec((tokens, height), lambda j: (0, 0))] * count
    specs.append(pl.BlockSpec((tokens, tile), lambda j: (0, j)))
    aliases = {}
    if earlier is not None:
        aliases = {len(ins): 0}
        ins.append(earlier)
        specs.append(pl.BlockSpec(memory_space=pl.ANY))
    for value in after:
        ins.append(value)
        specs.append(first_tile(value))

    def kernel(*refs):
        cols_ref = refs[count]
        out_ref, turned_ref = refs[-2:]

        @pl.when(pl.program_id(0) == 0)
        def _():
            for chunk in range(count):
                turned_ref[chunk * height : (chunk + 1) * height] = refs[chunk][...].T

        total = jnp.dot(turned_ref[...], cols_ref[...], preferred_element_type=F32)
        out_ref[...] = (total * scale).astype(BF16)

    return pl.pallas_call(
        kernel,
        out_shape=jax.ShapeDtypeStruct(shape, BF16),
        grid=(cols.shape[1] // tile,),
        in_specs=specs,
        out_specs=pl.BlockSpec((block, tile), lambda j: (index, j)),
        scratch_shapes=[pltpu.VMEM((block, tokens), BF16)],
        input_output_aliases=aliases,
        cost_estimate=cost(
            4 * block * cols.size, 2 * cols.size + 2 * block * (tokens + cols.shape[1])
        ),
        compiler_params=pltpu.CompilerParams(vmem_limit_bytes=48 * MIB),
        name="hessian_rows",
    )(*ins)


def add_pieces(pieces, after):
    rows, rank = pieces[0].shape

    def kernel(*refs):
        total = refs[0][...].astype(F32)
        for ref in refs[1 : len(pieces)]:
            total += ref[...].astype(F32)
        refs[-1][...] = total

    return pl.pallas_call(
        kernel,
        out_shape=jax.ShapeDtypeStruct((rows, rank), F32),
        grid=(1,),
        in_specs=[pl.BlockSpec(memory_space=pltpu.VMEM)] * len(pieces)
        + [first_tile(after)],
        out_specs=pl.BlockSpec(memory_space=pltpu.VMEM),
        cost_estimate=cost(0, 12 * rows * rank),
        name="add_pieces",
    )(*pieces, after)


def pair_sum(values):
    while len(values) > 1:
        values = [values[i] + values[i + 1] for i in range(0, len(values), 2)]
    return values[0]


def body(activations, weight_tile, codes, group_scales, right_factor):
    wide_count = lax.axis_size("wide")
    narrow_count = lax.axis_size("narrow")
    wide_index = lax.axis_index("wide").astype(jnp.int32)
    narrow_index = lax.axis_index("narrow").astype(jnp.int32)
    tokens, features = activations.shape
    rows = weight_tile.shape[0]
    split = features // rows
    scale = 1.0 / (tokens * wide_count)

    cols = lax.all_gather(activations, "wide", axis=0, tiled=True)

    right_block = lax.dynamic_slice_in_dim(right_factor, narrow_index * features, features, 0)
    own = jnp.dot(activations, right_block, preferred_element_type=F32)
    residual = residual_tile(weight_tile, codes, group_scales)

    height = rows // CHUNKS
    chunks = []
    tail = [own]
    after = []
    for chunk in range(CHUNKS):
        mine = take_chunk(activations, chunk, height, split, tail, after)
        blocks, sources = exchange_blocks(mine, [] if chunk else [residual])
        chunks.append((blocks, sources))
        tail = []
        after = [blocks[near] for near, _ in sources if near] + [residual]

    where = narrow_index.reshape(1)
    product = sum_tails(*chunks[0], where, height, [blocks[0] for blocks, _ in chunks[1:]])
    y = lax.all_gather(product, "wide", axis=0, tiled=True)
    y = y.reshape(tokens * wide_count, y.shape[2])
    hr, gram = hr_and_gram(cols, y, scale)

    row_chunks = []
    placed = []
    for chunk in range(CHUNKS):
        after = placed[-1:] + [hr] if chunk else []
        every = place_blocks(*chunks[chunk], where, height, after)
        placed.append(every)
        every = every.reshape(narrow_count * split, tokens, height)
        chunk_rows = lax.all_to_all(every, "wide", split_axis=0, concat_axis=0, tiled=True)
        row_chunks.append(chunk_rows.reshape(tokens * wide_count, height))

    partial = partial_product(residual, hr)
    share = rows // narrow_count
    received = []
    for m in range(narrow_count):
        piece = lax.dynamic_slice_in_dim(partial, (narrow_index ^ m) * share, share, 0)
        received.append(flip(piece, "narrow", m) if m else piece)

    hessian = None
    for chunk in range(CHUNKS):
        hessian = hessian_rows(
            [row_chunks[chunk]], cols, hessian, chunk, (rows, features), scale, [partial]
        )
    return add_pieces(received, hessian), gram, hessian


def solution(mesh):
    in_specs = (
        P("wide", "narrow"),
        P("wide", "narrow"),
        P("wide", "narrow"),
        P("wide", "narrow"),
        P(),
    )
    out_specs = (P(("wide", "narrow"), None), P(), P("wide", "narrow"))
    return jax.shard_map(body, mesh=mesh, in_specs=in_specs, out_specs=out_specs, check_vma=False)
```

```python
import functools

import jax
import jax.numpy as jnp
from jax import lax
from jax.experimental import pallas as pl
from jax.experimental.pallas import tpu as pltpu
from jax.sharding import PartitionSpec as P

CHUNKS = 2
MIB = 1024 * 1024
BF16 = jnp.bfloat16
F32 = jnp.float32


def flip(value, axis, mask):
    count = lax.axis_size(axis)
    return lax.ppermute(value, axis, [(i, i ^ mask) for i in range(count)])


def first_tile(value):
    shape = (1,) * (value.ndim - 2) + (16, 128)
    return pl.BlockSpec(shape, lambda *at: (0,) * value.ndim)


def cost(flops, moved):
    return pl.CostEstimate(flops=int(flops), bytes_accessed=int(moved), transcendentals=0)


def hr_and_gram(cols, y, scale):
    tokens, rank = y.shape
    features = cols.shape[1]
    tile = min(1024, features)

    def kernel(cols_ref, y_ref, hr_ref, gram_ref, turned_ref):
        @pl.when(pl.program_id(0) == 0)
        def _():
            turned_ref[...] = y_ref[...].T
            gram = jnp.dot(turned_ref[...], y_ref[...], preferred_element_type=F32)
            gram_ref[...] = gram * scale

        total = jnp.dot(turned_ref[...], cols_ref[...], preferred_element_type=F32) * scale
        hr_ref[...] = total.T.astype(BF16)

    return pl.pallas_call(
        kernel,
        out_shape=(
            jax.ShapeDtypeStruct((features, rank), BF16),
            jax.ShapeDtypeStruct((rank, rank), F32),
        ),
        grid=(features // tile,),
        in_specs=[
            pl.BlockSpec((tokens, tile), lambda j: (0, j)),
            pl.BlockSpec((tokens, rank), lambda j: (0, 0)),
        ],
        out_specs=(
            pl.BlockSpec((tile, rank), lambda j: (j, 0)),
            pl.BlockSpec((rank, rank), lambda j: (0, 0)),
        ),
        scratch_shapes=[pltpu.VMEM((rank, tokens), BF16)],
        cost_estimate=cost(4 * tokens * features * rank, 4 * cols.size),
        compiler_params=pltpu.CompilerParams(vmem_limit_bytes=48 * MIB),
        name="hr_and_gram",
    )(cols, y)


def place_kernel(sources, where_ref, *refs):
    out_ref = refs[-1]
    count = len(sources)
    me = where_ref[0]
    for mask in range(count):
        other = me ^ mask
        near, far = sources[mask]

        def put(index, other=other):
            out_ref[other] = refs[index][:, :, : out_ref.shape[3]]

        if far is None:
            put(near)
        elif near is None:
            put(far)
        else:
            close = jnp.abs(me - other) <= count // 2
            pl.when(close)(functools.partial(put, near))
            pl.when(jnp.logical_not(close))(functools.partial(put, far))


def place_blocks(blocks, sources, where, height, after):
    count = len(sources)
    return pl.pallas_call(
        functools.partial(place_kernel, sources),
        out_shape=jax.ShapeDtypeStruct((count,) + blocks[0].shape[:2] + (height,), BF16),
        grid=(1,),
        in_specs=[pl.BlockSpec(memory_space=pltpu.SMEM)]
        + [pl.BlockSpec(memory_space=pltpu.VMEM)] * len(blocks)
        + [first_tile(value) for value in after],
        out_specs=pl.BlockSpec(memory_space=pltpu.VMEM),
        cost_estimate=cost(0, 4 * count * blocks[0].size),
        compiler_params=pltpu.CompilerParams(vmem_limit_bytes=48 * MIB),
        name="place_blocks",
    )(where, *blocks, *after)


def take_chunk(activations, chunk, height, split, tail, after):
    tokens, features = activations.shape
    rows = features // split
    share = tail[0].shape[1] // split if tail else 0

    def kernel(activations_ref, *refs):
        for s in range(split):
            at = s * rows + chunk * height
            refs[-1][s, :, :height] = activations_ref[:, at : at + height]
            if tail:
                refs[-1][s, :, height:] = refs[0][:, s * share : (s + 1) * share].astype(BF16)

    shape = (split, tokens, height + share)
    return pl.pallas_call(
        kernel,
        out_shape=jax.ShapeDtypeStruct(shape, BF16),
        grid=(1,),
        in_specs=[pl.BlockSpec((tokens, features), lambda i: (0, 0))]
        + [pl.BlockSpec(value.shape, lambda i: (0, 0)) for value in tail]
        + [first_tile(value) for value in after],
        out_specs=pl.BlockSpec(shape, lambda i: (0, 0, 0)),
        cost_estimate=cost(0, 4 * split * tokens * height),
        name="take_chunk",
    )(activations, *tail, *after)


def sum_tails(blocks, sources, where, height, after):
    split, tokens, width = blocks[0].shape
    share = width - height
    count = len(sources)
    spec = pl.BlockSpec((split, tokens, share), lambda i: (0, 0, height // share))

    def kernel(where_ref, *refs):
        out_ref, held_ref = refs[-2:]
        me = where_ref[0]
        for mask in range(count):
            near, far = sources[mask]

            def put(index, mask=mask):
                held_ref[mask] = refs[index][...].astype(F32)

            if far is None:
                put(near)
            elif near is None:
                put(far)
            else:
                close = jnp.abs(me - (me ^ mask)) <= count // 2
                pl.when(close)(functools.partial(put, near))
                pl.when(jnp.logical_not(close))(functools.partial(put, far))
        total = pair_sum([held_ref[mask] for mask in range(count)])
        for s in range(split):
            out_ref[0, :, s * share : (s + 1) * share] = total[s].astype(BF16)

    return pl.pallas_call(
        kernel,
        out_shape=jax.ShapeDtypeStruct((1, tokens, split * share), BF16),
        grid=(1,),
        in_specs=[pl.BlockSpec(memory_space=pltpu.SMEM)]
        + [spec] * len(blocks)
        + [first_tile(value) for value in after],
        out_specs=pl.BlockSpec((1, tokens, split * share), lambda i: (0, 0, 0)),
        scratch_shapes=[pltpu.VMEM((count, split, tokens, share), F32)],
        cost_estimate=cost(0, 4 * count * split * tokens * share),
        name="sum_tails",
    )(where, *blocks, *after)


def relay(value, after):
    def kernel(value_ref, *refs):
        refs[-1][...] = value_ref[...]

    spec = pl.BlockSpec(value.shape, lambda i: (0, 0, 0))
    return pl.pallas_call(
        kernel,
        out_shape=jax.ShapeDtypeStruct(value.shape, value.dtype),
        grid=(1,),
        in_specs=[spec] + [first_tile(other) for other in after],
        out_specs=spec,
        cost_estimate=cost(0, 4 * value.size),
        name="relay",
    )(value, *after)


def exchange_blocks(mine, after):
    count = lax.axis_size("narrow")
    half = count // 2
    blocks = [mine]
    sources = [(0, None)]
    direct = {}
    order = sorted(range(1, count), key=lambda m: (m != half, m))
    for mask in order:
        pairs = [(i, i ^ mask) for i in range(count) if abs(i - (i ^ mask)) <= half]
        direct[mask] = lax.ppermute(mine, "narrow", pairs) if pairs else None
    onward = direct.get(half)
    if after and count > 2:
        onward = relay(onward, after)
    for mask in range(1, count):
        near = far = None
        if direct[mask] is not None:
            near = len(blocks)
            blocks.append(direct[mask])
        pairs = [(i ^ half, i ^ mask) for i in range(count) if abs(i - (i ^ mask)) > half]
        if pairs:
            far = len(blocks)
            blocks.append(lax.ppermute(onward, "narrow", pairs))
        sources.append((near, far))
    return blocks, sources


def residual_kernel(weight_ref, codes_ref, scales_ref, out_ref):
    groups = scales_ref.shape[1]
    width = weight_ref.shape[1] // groups
    scales = scales_ref[...]
    parts = []
    for group in range(groups):
        at = slice(group * width, (group + 1) * width)
        quantized = codes_ref[:, at].astype(F32) * scales[:, group : group + 1]
        parts.append((weight_ref[:, at].astype(F32) - quantized).astype(BF16))
    out_ref[...] = jnp.concatenate(parts, axis=1)


def residual_tile(weight, codes, scales):
    rows, features = weight.shape
    block = min(256, rows)
    return pl.pallas_call(
        residual_kernel,
        out_shape=jax.ShapeDtypeStruct((rows, features), BF16),
        grid=(rows // block,),
        in_specs=[
            pl.BlockSpec((block, features), lambda i: (i, 0)),
            pl.BlockSpec((block, features), lambda i: (i, 0)),
            pl.BlockSpec((block, scales.shape[1]), lambda i: (i, 0)),
        ],
        out_specs=pl.BlockSpec((block, features), lambda i: (i, 0)),
        compiler_params=pltpu.CompilerParams(vmem_limit_bytes=48 * MIB),
        cost_estimate=cost(0, 11 * rows * features),
        name="residual_tile",
    )(weight, codes, scales)


def product_kernel(residual_ref, hr_ref, out_ref):
    out_ref[...] = jnp.dot(residual_ref[...], hr_ref[...], preferred_element_type=F32).astype(BF16)


def partial_product(residual, hr):
    rows, features = residual.shape
    rank = hr.shape[1]
    block = min(512, rows)
    return pl.pallas_call(
        product_kernel,
        out_shape=jax.ShapeDtypeStruct((rows, rank), BF16),
        grid=(rows // block,),
        in_specs=[
            pl.BlockSpec((block, features), lambda i: (i, 0)),
            pl.BlockSpec((features, rank), lambda i: (0, 0)),
        ],
        out_specs=pl.BlockSpec((block, rank), lambda i: (i, 0)),
        compiler_params=pltpu.CompilerParams(vmem_limit_bytes=48 * MIB),
        cost_estimate=cost(4 * rows * features * rank, 3 * rows * features),
        name="partial_product",
    )(residual, hr)


def hessian_rows(row_chunks, cols, earlier, index, shape, scale, after):
    tokens, height = row_chunks[0].shape
    block = height * len(row_chunks)
    tile = min(1024, cols.shape[1])
    count = len(row_chunks)
    ins = [*row_chunks, cols]
    specs = [pl.BlockSpec((tokens, height), lambda j: (0, 0))] * count
    specs.append(pl.BlockSpec((tokens, tile), lambda j: (0, j)))
    aliases = {}
    if earlier is not None:
        aliases = {len(ins): 0}
        ins.append(earlier)
        specs.append(pl.BlockSpec(memory_space=pl.ANY))
    for value in after:
        ins.append(value)
        specs.append(first_tile(value))

    def kernel(*refs):
        cols_ref = refs[count]
        out_ref, turned_ref = refs[-2:]

        @pl.when(pl.program_id(0) == 0)
        def _():
            for chunk in range(count):
                turned_ref[chunk * height : (chunk + 1) * height] = refs[chunk][...].T

        total = jnp.dot(turned_ref[...], cols_ref[...], preferred_element_type=F32)
        out_ref[...] = (total * scale).astype(BF16)

    return pl.pallas_call(
        kernel,
        out_shape=jax.ShapeDtypeStruct(shape, BF16),
        grid=(cols.shape[1] // tile,),
        in_specs=specs,
        out_specs=pl.BlockSpec((block, tile), lambda j: (index, j)),
        scratch_shapes=[pltpu.VMEM((block, tokens), BF16)],
        input_output_aliases=aliases,
        cost_estimate=cost(
            4 * block * cols.size, 2 * cols.size + 2 * block * (tokens + cols.shape[1])
        ),
        compiler_params=pltpu.CompilerParams(vmem_limit_bytes=48 * MIB),
        name="hessian_rows",
    )(*ins)


def add_pieces(pieces, after):
    rows, rank = pieces[0].shape

    def kernel(*refs):
        total = refs[0][...].astype(F32)
        for ref in refs[1 : len(pieces)]:
            total += ref[...].astype(F32)
        refs[-1][...] = total

    return pl.pallas_call(
        kernel,
        out_shape=jax.ShapeDtypeStruct((rows, rank), F32),
        grid=(1,),
        in_specs=[pl.BlockSpec(memory_space=pltpu.VMEM)] * len(pieces)
        + [first_tile(after)],
        out_specs=pl.BlockSpec(memory_space=pltpu.VMEM),
        cost_estimate=cost(0, 12 * rows * rank),
        name="add_pieces",
    )(*pieces, after)


def pair_sum(values):
    while len(values) > 1:
        values = [values[i] + values[i + 1] for i in range(0, len(values), 2)]
    return values[0]


def body(activations, weight_tile, codes, group_scales, right_factor):
    wide_count = lax.axis_size("wide")
    narrow_count = lax.axis_size("narrow")
    wide_index = lax.axis_index("wide").astype(jnp.int32)
    narrow_index = lax.axis_index("narrow").astype(jnp.int32)
    tokens, features = activations.shape
    rows = weight_tile.shape[0]
    split = features // rows
    scale = 1.0 / (tokens * wide_count)

    cols = lax.all_gather(activations, "wide", axis=0, tiled=True)

    right_block = lax.dynamic_slice_in_dim(right_factor, narrow_index * features, features, 0)
    own = jnp.dot(activations, right_block, preferred_element_type=F32)
    residual = residual_tile(weight_tile, codes, group_scales)

    height = rows // CHUNKS
    chunks = []
    tail = [own]
    after = []
    for chunk in range(CHUNKS):
        mine = take_chunk(activations, chunk, height, split, tail, after)
        blocks, sources = exchange_blocks(mine, [] if chunk else [residual])
        chunks.append((blocks, sources))
        tail = []
        after = [blocks[near] for near, _ in sources if near] + [residual]

    where = narrow_index.reshape(1)
    later, later_at = chunks[1]
    direct = [later[near] for near, _ in later_at if near]
    product = sum_tails(*chunks[0], where, height, [later[0]] + direct[-1:])
    y = lax.all_gather(product, "wide", axis=0, tiled=True)
    y = y.reshape(tokens * wide_count, y.shape[2])
    hr, gram = hr_and_gram(cols, y, scale)

    row_chunks = []
    placed = []
    for chunk in range(CHUNKS):
        after = placed[-1:] + [hr] if chunk else [product]
        every = place_blocks(*chunks[chunk], where, height, after)
        placed.append(every)
        every = every.reshape(narrow_count * split, tokens, height)
        chunk_rows = lax.all_to_all(every, "wide", split_axis=0, concat_axis=0, tiled=True)
        row_chunks.append(chunk_rows.reshape(tokens * wide_count, height))

    partial = partial_product(residual, hr)
    share = rows // narrow_count
    received = []
    for m in range(narrow_count):
        piece = lax.dynamic_slice_in_dim(partial, (narrow_index ^ m) * share, share, 0)
        received.append(flip(piece, "narrow", m) if m else piece)

    hessian = None
    for chunk in range(CHUNKS):
        hessian = hessian_rows(
            [row_chunks[chunk]], cols, hessian, chunk, (rows, features), scale, [partial]
        )
    return add_pieces(received, hessian), gram, hessian


def solution(mesh):
    in_specs = (
        P("wide", "narrow"),
        P("wide", "narrow"),
        P("wide", "narrow"),
        P("wide", "narrow"),
        P(),
    )
    out_specs = (P(("wide", "narrow"), None), P(), P("wide", "narrow"))
    return jax.shard_map(body, mesh=mesh, in_specs=in_specs, out_specs=out_specs, check_vma=False)
```

```python
import functools

import jax
import jax.numpy as jnp
from jax import lax
from jax.experimental import pallas as pl
from jax.experimental.pallas import tpu as pltpu
from jax.sharding import PartitionSpec as P

CHUNKS = 2
MIB = 1024 * 1024
BF16 = jnp.bfloat16
F32 = jnp.float32


def flip(value, axis, mask):
    count = lax.axis_size(axis)
    return lax.ppermute(value, axis, [(i, i ^ mask) for i in range(count)])


def first_tile(value):
    shape = (1,) * (value.ndim - 2) + (16, 128)
    return pl.BlockSpec(shape, lambda *at: (0,) * value.ndim)


def cost(flops, moved):
    return pl.CostEstimate(flops=int(flops), bytes_accessed=int(moved), transcendentals=0)


def hr_and_gram(cols, y, scale):
    tokens, rank = y.shape
    features = cols.shape[1]
    tile = min(1024, features)

    def kernel(cols_ref, y_ref, hr_ref, gram_ref, turned_ref):
        @pl.when(pl.program_id(0) == 0)
        def _():
            turned_ref[...] = y_ref[...].T
            gram = jnp.dot(turned_ref[...], y_ref[...], preferred_element_type=F32)
            gram_ref[...] = gram * scale

        total = jnp.dot(turned_ref[...], cols_ref[...], preferred_element_type=F32) * scale
        hr_ref[...] = total.T.astype(BF16)

    return pl.pallas_call(
        kernel,
        out_shape=(
            jax.ShapeDtypeStruct((features, rank), BF16),
            jax.ShapeDtypeStruct((rank, rank), F32),
        ),
        grid=(features // tile,),
        in_specs=[
            pl.BlockSpec((tokens, tile), lambda j: (0, j)),
            pl.BlockSpec((tokens, rank), lambda j: (0, 0)),
        ],
        out_specs=(
            pl.BlockSpec((tile, rank), lambda j: (j, 0)),
            pl.BlockSpec((rank, rank), lambda j: (0, 0)),
        ),
        scratch_shapes=[pltpu.VMEM((rank, tokens), BF16)],
        cost_estimate=cost(4 * tokens * features * rank, 4 * cols.size),
        compiler_params=pltpu.CompilerParams(vmem_limit_bytes=48 * MIB),
        name="hr_and_gram",
    )(cols, y)


def place_kernel(sources, where_ref, *refs):
    out_ref = refs[-1]
    count = len(sources)
    me = where_ref[0]
    for mask in range(count):
        other = me ^ mask
        near, far = sources[mask]

        def put(index, other=other):
            out_ref[other] = refs[index][:, :, : out_ref.shape[3]]

        if far is None:
            put(near)
        elif near is None:
            put(far)
        else:
            close = jnp.abs(me - other) <= count // 2
            pl.when(close)(functools.partial(put, near))
            pl.when(jnp.logical_not(close))(functools.partial(put, far))


def place_blocks(blocks, sources, where, height, after):
    count = len(sources)
    return pl.pallas_call(
        functools.partial(place_kernel, sources),
        out_shape=jax.ShapeDtypeStruct((count,) + blocks[0].shape[:2] + (height,), BF16),
        grid=(1,),
        in_specs=[pl.BlockSpec(memory_space=pltpu.SMEM)]
        + [pl.BlockSpec(memory_space=pltpu.VMEM)] * len(blocks)
        + [first_tile(value) for value in after],
        out_specs=pl.BlockSpec(memory_space=pltpu.VMEM),
        cost_estimate=cost(0, 4 * count * blocks[0].size),
        compiler_params=pltpu.CompilerParams(vmem_limit_bytes=48 * MIB),
        name="place_blocks",
    )(where, *blocks, *after)


def take_chunk(activations, chunk, height, split, tail, after):
    tokens, features = activations.shape
    rows = features // split
    share = tail[0].shape[1] // split if tail else 0

    def kernel(activations_ref, *refs):
        for s in range(split):
            at = s * rows + chunk * height
            refs[-1][s, :, :height] = activations_ref[:, at : at + height]
            if tail:
                refs[-1][s, :, height:] = refs[0][:, s * share : (s + 1) * share].astype(BF16)

    shape = (split, tokens, height + share)
    return pl.pallas_call(
        kernel,
        out_shape=jax.ShapeDtypeStruct(shape, BF16),
        grid=(1,),
        in_specs=[pl.BlockSpec((tokens, features), lambda i: (0, 0))]
        + [pl.BlockSpec(value.shape, lambda i: (0, 0)) for value in tail]
        + [first_tile(value) for value in after],
        out_specs=pl.BlockSpec(shape, lambda i: (0, 0, 0)),
        cost_estimate=cost(0, 4 * split * tokens * height),
        name="take_chunk",
    )(activations, *tail, *after)


def sum_tails(blocks, sources, where, height, after):
    split, tokens, width = blocks[0].shape
    share = width - height
    count = len(sources)
    spec = pl.BlockSpec((split, tokens, share), lambda i: (0, 0, height // share))

    def kernel(where_ref, *refs):
        out_ref, held_ref = refs[-2:]
        me = where_ref[0]
        for mask in range(count):
            near, far = sources[mask]

            def put(index, mask=mask):
                held_ref[mask] = refs[index][...].astype(F32)

            if far is None:
                put(near)
            elif near is None:
                put(far)
            else:
                close = jnp.abs(me - (me ^ mask)) <= count // 2
                pl.when(close)(functools.partial(put, near))
                pl.when(jnp.logical_not(close))(functools.partial(put, far))
        total = pair_sum([held_ref[mask] for mask in range(count)])
        for s in range(split):
            out_ref[0, :, s * share : (s + 1) * share] = total[s].astype(BF16)

    return pl.pallas_call(
        kernel,
        out_shape=jax.ShapeDtypeStruct((1, tokens, split * share), BF16),
        grid=(1,),
        in_specs=[pl.BlockSpec(memory_space=pltpu.SMEM)]
        + [spec] * len(blocks)
        + [first_tile(value) for value in after],
        out_specs=pl.BlockSpec((1, tokens, split * share), lambda i: (0, 0, 0)),
        scratch_shapes=[pltpu.VMEM((count, split, tokens, share), F32)],
        cost_estimate=cost(0, 4 * count * split * tokens * share),
        name="sum_tails",
    )(where, *blocks, *after)


def relay(value, after):
    def kernel(value_ref, *refs):
        refs[-1][...] = value_ref[...]

    spec = pl.BlockSpec(value.shape, lambda i: (0, 0, 0))
    return pl.pallas_call(
        kernel,
        out_shape=jax.ShapeDtypeStruct(value.shape, value.dtype),
        grid=(1,),
        in_specs=[spec] + [first_tile(other) for other in after],
        out_specs=spec,
        cost_estimate=cost(0, 4 * value.size),
        name="relay",
    )(value, *after)


def exchange_blocks(mine, after):
    count = lax.axis_size("narrow")
    half = count // 2
    blocks = [mine]
    sources = [(0, None)]
    direct = {}
    order = sorted(range(1, count), key=lambda m: (m != half, m))
    for mask in order:
        pairs = [(i, i ^ mask) for i in range(count) if abs(i - (i ^ mask)) <= half]
        direct[mask] = lax.ppermute(mine, "narrow", pairs) if pairs else None
    onward = direct.get(half)
    if after and count > 2:
        onward = relay(onward, after)
    for mask in range(1, count):
        near = far = None
        if direct[mask] is not None:
            near = len(blocks)
            blocks.append(direct[mask])
        pairs = [(i ^ half, i ^ mask) for i in range(count) if abs(i - (i ^ mask)) > half]
        if pairs:
            far = len(blocks)
            blocks.append(lax.ppermute(onward, "narrow", pairs))
        sources.append((near, far))
    return blocks, sources


def residual_kernel(weight_ref, codes_ref, scales_ref, out_ref):
    groups = scales_ref.shape[1]
    width = weight_ref.shape[1] // groups
    scales = scales_ref[...]
    parts = []
    for group in range(groups):
        at = slice(group * width, (group + 1) * width)
        quantized = codes_ref[:, at].astype(F32) * scales[:, group : group + 1]
        parts.append((weight_ref[:, at].astype(F32) - quantized).astype(BF16))
    out_ref[...] = jnp.concatenate(parts, axis=1)


def residual_tile(weight, codes, scales):
    rows, features = weight.shape
    block = min(256, rows)
    return pl.pallas_call(
        residual_kernel,
        out_shape=jax.ShapeDtypeStruct((rows, features), BF16),
        grid=(rows // block,),
        in_specs=[
            pl.BlockSpec((block, features), lambda i: (i, 0)),
            pl.BlockSpec((block, features), lambda i: (i, 0)),
            pl.BlockSpec((block, scales.shape[1]), lambda i: (i, 0)),
        ],
        out_specs=pl.BlockSpec((block, features), lambda i: (i, 0)),
        compiler_params=pltpu.CompilerParams(vmem_limit_bytes=48 * MIB),
        cost_estimate=cost(0, 11 * rows * features),
        name="residual_tile",
    )(weight, codes, scales)


def product_kernel(residual_ref, hr_ref, out_ref):
    out_ref[...] = jnp.dot(residual_ref[...], hr_ref[...], preferred_element_type=F32).astype(BF16)


def partial_product(residual, hr):
    rows, features = residual.shape
    rank = hr.shape[1]
    block = min(512, rows)
    return pl.pallas_call(
        product_kernel,
        out_shape=jax.ShapeDtypeStruct((rows, rank), BF16),
        grid=(rows // block,),
        in_specs=[
            pl.BlockSpec((block, features), lambda i: (i, 0)),
            pl.BlockSpec((features, rank), lambda i: (0, 0)),
        ],
        out_specs=pl.BlockSpec((block, rank), lambda i: (i, 0)),
        compiler_params=pltpu.CompilerParams(vmem_limit_bytes=48 * MIB),
        cost_estimate=cost(4 * rows * features * rank, 3 * rows * features),
        name="partial_product",
    )(residual, hr)


def hessian_rows(row_chunks, cols, earlier, index, shape, scale, after):
    tokens, height = row_chunks[0].shape
    block = height * len(row_chunks)
    tile = min(1024, cols.shape[1])
    count = len(row_chunks)
    ins = [*row_chunks, cols]
    specs = [pl.BlockSpec((tokens, height), lambda j: (0, 0))] * count
    specs.append(pl.BlockSpec((tokens, tile), lambda j: (0, j)))
    aliases = {}
    if earlier is not None:
        aliases = {len(ins): 0}
        ins.append(earlier)
        specs.append(pl.BlockSpec(memory_space=pl.ANY))
    for value in after:
        ins.append(value)
        specs.append(first_tile(value))

    def kernel(*refs):
        cols_ref = refs[count]
        out_ref, turned_ref = refs[-2:]

        @pl.when(pl.program_id(0) == 0)
        def _():
            for chunk in range(count):
                turned_ref[chunk * height : (chunk + 1) * height] = refs[chunk][...].T

        total = jnp.dot(turned_ref[...], cols_ref[...], preferred_element_type=F32)
        out_ref[...] = (total * scale).astype(BF16)

    return pl.pallas_call(
        kernel,
        out_shape=jax.ShapeDtypeStruct(shape, BF16),
        grid=(cols.shape[1] // tile,),
        in_specs=specs,
        out_specs=pl.BlockSpec((block, tile), lambda j: (index, j)),
        scratch_shapes=[pltpu.VMEM((block, tokens), BF16)],
        input_output_aliases=aliases,
        cost_estimate=cost(
            4 * block * cols.size, 2 * cols.size + 2 * block * (tokens + cols.shape[1])
        ),
        compiler_params=pltpu.CompilerParams(vmem_limit_bytes=48 * MIB),
        name="hessian_rows",
    )(*ins)


def add_pieces(pieces, after):
    rows, rank = pieces[0].shape

    def kernel(*refs):
        total = refs[0][...].astype(F32)
        for ref in refs[1 : len(pieces)]:
            total += ref[...].astype(F32)
        refs[-1][...] = total

    return pl.pallas_call(
        kernel,
        out_shape=jax.ShapeDtypeStruct((rows, rank), F32),
        grid=(1,),
        in_specs=[pl.BlockSpec(memory_space=pltpu.VMEM)] * len(pieces)
        + [first_tile(after)],
        out_specs=pl.BlockSpec(memory_space=pltpu.VMEM),
        cost_estimate=cost(0, 12 * rows * rank),
        name="add_pieces",
    )(*pieces, after)


def pair_sum(values):
    while len(values) > 1:
        values = [values[i] + values[i + 1] for i in range(0, len(values), 2)]
    return values[0]


def body(activations, weight_tile, codes, group_scales, right_factor):
    wide_count = lax.axis_size("wide")
    narrow_count = lax.axis_size("narrow")
    wide_index = lax.axis_index("wide").astype(jnp.int32)
    narrow_index = lax.axis_index("narrow").astype(jnp.int32)
    tokens, features = activations.shape
    rows = weight_tile.shape[0]
    split = features // rows
    scale = 1.0 / (tokens * wide_count)

    cols = lax.all_gather(activations, "wide", axis=0, tiled=True)

    right_block = lax.dynamic_slice_in_dim(right_factor, narrow_index * features, features, 0)
    own = jnp.dot(activations, right_block, preferred_element_type=F32)
    residual = residual_tile(weight_tile, codes, group_scales)

    height = rows // CHUNKS
    chunks = []
    tail = [own]
    after = []
    for chunk in range(CHUNKS):
        mine = take_chunk(activations, chunk, height, split, tail, after)
        blocks, sources = exchange_blocks(mine, [] if chunk else [residual])
        chunks.append((blocks, sources))
        tail = []
        after = [blocks[near] for near, _ in sources if near] + [residual]

    where = narrow_index.reshape(1)
    later, later_at = chunks[1]
    halfway = later[later_at[narrow_count // 2][0]]
    product = sum_tails(*chunks[0], where, height, [later[0], halfway])
    y = lax.all_gather(product, "wide", axis=0, tiled=True)
    y = y.reshape(tokens * wide_count, y.shape[2])
    hr, gram = hr_and_gram(cols, y, scale)

    row_chunks = []
    placed = []
    for chunk in range(CHUNKS):
        after = placed[-1:] + [hr] if chunk else [product]
        every = place_blocks(*chunks[chunk], where, height, after)
        placed.append(every)
        every = every.reshape(narrow_count * split, tokens, height)
        chunk_rows = lax.all_to_all(every, "wide", split_axis=0, concat_axis=0, tiled=True)
        row_chunks.append(chunk_rows.reshape(tokens * wide_count, height))

    partial = partial_product(residual, hr)
    share = rows // narrow_count
    received = []
    for m in range(narrow_count):
        piece = lax.dynamic_slice_in_dim(partial, (narrow_index ^ m) * share, share, 0)
        received.append(flip(piece, "narrow", m) if m else piece)

    hessian = None
    for chunk in range(CHUNKS):
        hessian = hessian_rows(
            [row_chunks[chunk]], cols, hessian, chunk, (rows, features), scale, [partial]
        )
    return add_pieces(received, hessian), gram, hessian


def solution(mesh):
    in_specs = (
        P("wide", "narrow"),
        P("wide", "narrow"),
        P("wide", "narrow"),
        P("wide", "narrow"),
        P(),
    )
    out_specs = (P(("wide", "narrow"), None), P(), P("wide", "narrow"))
    return jax.shard_map(body, mesh=mesh, in_specs=in_specs, out_specs=out_specs, check_vma=False)
```
